256 devices in a mesh: grp: 16 (over z, core), blk: 16 (over x, y).
Axes of the slice: x: 4, y: 4, z: 8, core: 2. Of those that a mesh axis runs over, the one named last changes fastest.
Arguments:
- block_tiles: bfloat16 [512, 32, 256, 256], P(('grp', 'blk')), may hold values from -0.0625 to 0.0625
- col_blocks: int32 [512, 32], P(('grp', 'blk')), may hold values from 0 to 511, as said below
- scales: float32 [512, 32], P(('grp', 'blk')), may hold values from 0.5 to 2
- x_start: float32 [32, 131072], P(None, ('grp', 'blk')), may hold values from -6 to 6
- p_start: float32 [32, 131072], P(None, ('grp', 'blk')), may hold values from -6 to 6
Outputs:
- x_next: float32 [32, 131072], P(None, ('grp', 'blk'))
- p_next: float32 [32, 131072], P(None, ('grp', 'blk'))
The draws below stay inside these ranges and needn't reach their ends.
Inputs may be any that keep to these rules, and one draw needn't show every extreme that they name: col_blocks[b, 0] = b. With g = b // 32: entries 1 to 23 of row b lie in block rows g * 32 to (g + 1) * 32 - 1; entries 3 * 8 to 27 lie in the block rows of cluster (g - 1) modulo 16; entries 7 * 4 to 31 lie in those of cluster (g + 1) modulo 16.
All inputs are finite; a program needn't handle non-finite values.
Results may differ from the reference program's by a relative error of at most 0.003.
Values may be sent and summed in bfloat16 or wider, within the bound.
A program may use at most 64 MiB of HBM per device.

```python
import math
import jax
import jax.numpy as jnp
from jax import lax

BLOCK = 256
KB = 32
K = 32
NS_STEPS = 8
GROUP_BLOCKS = 32
NB = 512
N = 131072
N_GRP = 16


def draw_col_blocks(key, part):
    row_index = jnp.arange(NB, dtype=jnp.int32)
    group_of = row_index // GROUP_BLOCKS
    slot_index = jnp.arange(KB, dtype=jnp.int32)
    inner_count = 3 * KB // 4
    outer_count = (KB - inner_count) // 2
    group_step = jnp.where(slot_index < inner_count, 0, jnp.where(slot_index < inner_count + outer_count, N_GRP - 1, 1)).astype(jnp.int32)
    target_group = (group_of[:, None] + group_step[None, :]) % N_GRP
    offset_draw = jax.random.randint(key, (NB, KB), 0, GROUP_BLOCKS, dtype=jnp.int32)
    chosen = target_group * GROUP_BLOCKS + offset_draw
    return jnp.where(slot_index[None, :] == 0, row_index[:, None], chosen).astype(jnp.int32)


def shard_levels(own_key, dims, shards, smallest, top_value):
    loudness, own = 1.0, jax.random.fold_in(own_key, 6)
    for axis_at, blocks in shards:
        draws = jnp.exp(jax.random.uniform(jax.random.fold_in(own, axis_at), (blocks,), jnp.float32, smallest / len(shards), top_value / len(shards)))
        loudness = loudness * jnp.repeat(draws, dims[axis_at] // blocks).reshape([-1 if axis == axis_at else 1 for axis in range(len(dims))])
    return loudness


def scatter_about(key, dims, spread, reach, pieces=(), held_as=jnp.bfloat16):
    loudness = shard_levels(key, dims, pieces, -0.22, 0.18) if pieces else 1.0
    values = jax.random.normal(key, dims, jnp.float32) * spread * loudness
    return jnp.minimum(jnp.maximum(values, -reach), reach).astype(held_as)


def setup_inputs(seed: int = 0) -> dict:
    seeds = jax.random.split(jax.random.key(seed), 6)
    block_tiles = scatter_about(seeds[0], (NB, KB, BLOCK, BLOCK), (KB * BLOCK) ** -0.5, 0.0625, ((0, 256),))
    col_blocks = draw_col_blocks(jax.random.fold_in(seeds[5], 71), 0)
    scales = jnp.clip(jnp.exp(math.log(2.0) - 1.3862944 * jax.random.uniform(seeds[2], (NB, KB), jnp.float32) ** shard_levels(seeds[2], (NB, KB), ((0, 256),), -0.2, 0.2)), 0.5, 2.0)
    x_start = scatter_about(seeds[3], (K, N), 1.0, 6.0, ((1, 256),), jnp.float32)
    p_start = scatter_about(seeds[4], (K, N), 1.0, 6.0, ((1, 256),), jnp.float32)
    return dict(block_tiles=block_tiles, col_blocks=col_blocks, scales=scales, x_start=x_start, p_start=p_start)


def lower_solve(factor, rhs, transposed=False):
    return lax.linalg.triangular_solve(factor, rhs, left_side=True, lower=True, transpose_a=transposed)

def apply_laplacian(field, block_tiles, col_blocks, scales):
    width_rows = field.shape[0]
    rounded = field.astype(jnp.bfloat16)
    rounded = lax.optimization_barrier(rounded).astype(jnp.float32)
    blocks = rounded.reshape(width_rows, NB, BLOCK)

    def one_row(entries):
        tile_block, col_row, scale_row = entries
        picked = jnp.take(blocks, col_row, axis=1)
        products = jnp.einsum('wjc,jrc->jwr', picked, tile_block.astype(jnp.float32), precision=lax.Precision.HIGHEST)
        return jnp.einsum('jwr,j->wr', products, scale_row, precision=lax.Precision.HIGHEST)
    mixture = lax.map(one_row, (block_tiles, col_blocks, scales))
    return field - jnp.transpose(mixture, (1, 0, 2)).reshape(width_rows, NB * BLOCK)

def spectral_filter(ritz_matrix):
    order_size = ritz_matrix.shape[0]
    identity = jnp.eye(order_size, dtype=jnp.float32)
    spectral_shift = jnp.trace(ritz_matrix) / order_size
    centred = spectral_shift * identity - ritz_matrix
    iterate = centred / jnp.sqrt(jnp.sum(centred * centred) + 1e-06)
    for repeat in range(NS_STEPS):
        cubed = jnp.dot(iterate, jnp.dot(iterate, iterate, precision=lax.Precision.HIGHEST), precision=lax.Precision.HIGHEST)
        iterate = 1.5 * iterate - 0.5 * cubed
    return 0.5 * (identity + iterate)

def reference(block_tiles, col_blocks, scales, x_start, p_start):
    high = lax.Precision.HIGHEST
    item_count = x_start.shape[1]
    image_x = apply_laplacian(x_start, block_tiles, col_blocks, scales)
    image_p = apply_laplacian(p_start, block_tiles, col_blocks, scales)
    gram_x = jnp.dot(x_start, x_start.T, precision=high) / item_count
    cross_x = jnp.dot(x_start, image_x.T, precision=high) / item_count
    chol_x = jnp.linalg.cholesky(gram_x)
    coupling = lower_solve(chol_x, lower_solve(chol_x, cross_x), True)
    residual = image_x - jnp.dot(coupling.T, x_start, precision=high)
    image_r = apply_laplacian(residual, block_tiles, col_blocks, scales)
    full_basis = jnp.concatenate([x_start, residual, p_start], axis=0)
    images = jnp.concatenate([image_x, image_r, image_p], axis=0)
    gram_basis = jnp.dot(full_basis, full_basis.T, precision=high) / item_count
    projected = jnp.dot(full_basis, images.T, precision=high) / item_count
    chol_lower = jnp.linalg.cholesky(gram_basis)
    half_solved = lower_solve(chol_lower, projected)
    ritz_matrix = lower_solve(chol_lower, half_solved.T)
    ritz_matrix = 0.5 * (ritz_matrix + ritz_matrix.T)
    filtered = spectral_filter(ritz_matrix)
    coefficients = lower_solve(chol_lower, filtered[:, :K], True)
    new_x = jnp.dot(coefficients.T, full_basis, precision=high)
    new_p = jnp.dot(coefficients[K:].T, full_basis[K:], precision=high)
    gram_new = jnp.dot(new_x, new_x.T, precision=high) / item_count
    chol_new = jnp.linalg.cholesky(gram_new)
    x_next = lower_solve(chol_new, new_x)
    p_next = lower_solve(chol_new, new_p)
    return (x_next, p_next)
```

```python
import functools

import jax
import jax.numpy as jnp
from jax import lax
from jax.experimental import pallas as pl
from jax.experimental.pallas import tpu as pltpu
from jax.sharding import PartitionSpec as P

NS_STEPS = 8
PANEL = 8
HIGH = lax.Precision.HIGHEST
F32 = jnp.float32
BF16 = jnp.bfloat16


def dot_nt(a, b, precision=None):
    return lax.dot_general(
        a, b, (((1,), (1,)), ((), ())), precision=precision, preferred_element_type=F32
    )


def dot_nn(a, b, precision=HIGH):
    return jnp.dot(a, b, precision=precision, preferred_element_type=F32)


def collect(
    n_grp,
    n_blk,
    side,
    cols_hbm,
    scales_hbm,
    x_hbm,
    p_hbm,
    tiles_hbm,
    gram_ref,
    image_ref,
    s_ref,
    cols,
    scales,
    x_ref,
    p_ref,
    tiles,
    x_panel,
    p_panel,
    s_panel,
    want_next,
    want_prev,
    x_out,
    x_in,
    p_out,
    p_in,
    s_out,
    s_in,
    partial,
    rs_buf,
    ar_buf,
    mine_t,
    mate_t,
    blk_t,
    z_t,
    load_sem,
    ask_send,
    ask_recv,
    x_send,
    x_recv,
    p_send,
    p_recv,
    p_send2,
    p_recv2,
    s_send,
    s_recv,
    z_send,
    z_recv,
    rs_send,
    rs_recv,
    ar_send,
    ar_recv,
    ag_send,
    ag_recv,
    mate_send,
    mate_recv,
    blk_send,
    blk_recv,
    zt_send,
    zt_recv,
):
    me_g = lax.axis_index("grp")
    me_b = lax.axis_index("blk")
    me_x, me_y = me_b // side, lax.rem(me_b, side)
    nxt = lax.rem(me_g + 1, n_grp)
    prv = lax.rem(me_g + n_grp - 1, n_grp)
    core = lax.rem(me_g, 2)
    mate = me_g + 1 - 2 * core
    rows_here, slots = cols.shape
    k = x_ref.shape[0]
    width = tiles.shape[2]
    cluster = n_blk * rows_here
    inner = 3 * slots // 4
    outer = slots // 8
    n_early = 3 * k // 8
    half = k // 2

    def load(src, dst, i):
        return pltpu.make_async_copy(src, dst, load_sem.at[i])

    load_x, load_p = load(x_hbm, x_ref, 0), load(p_hbm, p_ref, 1)
    load_small = [load(cols_hbm, cols, 2), load(scales_hbm, scales, 3)]
    load_tiles = [load(tiles_hbm.at[i], tiles.at[i], 4 + i) for i in range(rows_here)]
    for copy in [load_x, load_p, *load_small, *load_tiles]:
        copy.start()

    barrier = pltpu.get_barrier_semaphore()

    def greet(grp, blk):
        pl.semaphore_signal(
            barrier, inc=1, device_id=(grp, blk), device_id_type=pl.DeviceIdType.MESH
        )

    def greet_blk(d, c):
        greet(me_g, lax.rem(me_b + d, n_blk))
        return c

    def greet_grp(d, c):
        greet(lax.rem(me_g + d, n_grp), me_b)
        return c

    lax.fori_loop(1, n_blk, greet_blk, 0)
    lax.fori_loop(1, n_grp, greet_grp, 0)

    def block(ref, i):
        return ref[:, i * width : (i + 1) * width].astype(BF16)

    load_x.wait()
    for i in range(rows_here):
        x_panel[i, me_x, me_y] = block(x_ref, i)
    load_p.wait()
    for i in range(rows_here):
        p_panel[i, me_x, me_y] = block(p_ref, i)
    for copy in load_small:
        copy.wait()
    pl.semaphore_wait(barrier, n_blk - 1 + n_grp - 1)

    def remote(src, dst, send, recv, grp, blk):
        return pltpu.make_async_remote_copy(
            src_ref=src,
            dst_ref=dst,
            send_sem=send,
            recv_sem=recv,
            device_id=(grp, blk),
            device_id_type=pl.DeviceIdType.MESH,
        )

    ask = [
        remote(cols, want_next, ask_send.at[0], ask_recv.at[0], prv, me_b),
        remote(cols, want_prev, ask_send.at[1], ask_recv.at[1], nxt, me_b),
    ]

    def each(count, act):
        def body(d, c):
            act(d)
            return c

        lax.fori_loop(1, count, body, 0)

    def along_x(d):
        return lax.rem(me_x + d, side) * side + me_y

    def along_y(d):
        return me_x * side + lax.rem(me_y + d, side)

    def p_first(d):
        a, b = p_panel.at[0, me_x, me_y], p_panel.at[1, me_x, me_y]
        return [
            remote(a, a, p_send.at[0, d], p_recv.at[0, d], me_g, along_x(d)),
            remote(b, b, p_send.at[1, d], p_recv.at[1, d], me_g, along_y(d)),
        ]

    def p_second(d):
        a, b = p_panel.at[0, :, me_y], p_panel.at[1, me_x]
        return [
            remote(a, a, p_send2.at[0, d], p_recv2.at[0, d], me_g, along_y(d)),
            remote(b, b, p_send2.at[1, d], p_recv2.at[1, d], me_g, along_x(d)),
        ]

    def near(buf, send, recv, d):
        a, b = buf.at[0, me_x, me_y], buf.at[1, me_x, me_y]
        return [
            remote(a, a, send.at[0, side, d], recv.at[0, side, d], me_g, along_x(d)),
            remote(b, b, send.at[1, side, d], recv.at[1, side, d], me_g, along_y(d)),
        ]

    def onward(buf, send, recv, e, d):
        from_x, from_y = lax.rem(me_x + side - e, side), lax.rem(me_y + side - e, side)
        a, b = buf.at[0, from_x, me_y], buf.at[1, me_x, from_y]
        return [
            remote(a, a, send.at[0, e, d], recv.at[0, e, d], me_g, along_y(d)),
            remote(b, b, send.at[1, e, d], recv.at[1, e, d], me_g, along_x(d)),
        ]

    def start(copies):
        for copy in copies:
            copy.start()

    def wait(copies):
        for copy in copies:
            copy.wait()

    def send_own(buf, send, recv):
        each(side, lambda d: start(near(buf, send, recv, d)))
        each(side, lambda d: start(onward(buf, send, recv, 0, d)))

    def pass_on(buf, send, recv):
        def arrived(e):
            for copy in near(buf, send, recv, e):
                copy.wait_recv()
            each(side, lambda d: start(onward(buf, send, recv, e, d)))

        each(side, arrived)

    def all_in(buf, send, recv):
        def sent(d):
            for copy in near(buf, send, recv, d):
                copy.wait_send()
            wait(onward(buf, send, recv, 0, d))

        each(side, sent)
        each(side, lambda e: each(side, lambda d: wait(onward(buf, send, recv, e, d))))

    def crossed(buf):
        def get(c):
            c = lax.rem(c, cluster)
            at = c // rows_here
            return buf[lax.rem(c, rows_here), at // side, lax.rem(at, side)]

        return get

    def exchange(out, into, at):
        return [
            remote(out.at[0], into.at[0], z_send.at[at], z_recv.at[at], nxt, me_b),
            remote(out.at[1], into.at[1], z_send.at[at + 1], z_recv.at[at + 1], prv, me_b),
        ]

    def pick(get, out):
        for i in range(rows_here):
            for j in range(outer):
                out[0, i * outer + j] = get(want_next[i, inner + j])
                out[1, i * outer + j] = get(want_prev[i, inner + outer + j])

    def mix_inner(get):
        sums = []
        for i in range(rows_here):

            def body(j, acc, i=i):
                return acc + dot_nt(get(cols[i, j]), tiles[i, j]) * scales[i, j]

            sums.append(lax.fori_loop(0, inner, body, jnp.zeros((k, width), F32), unroll=8))
        return sums

    def mix_outer(sums, into):
        for i in range(rows_here):
            for j in range(outer):
                a, b = inner + j, inner + outer + j
                sums[i] += dot_nt(into[0, i * outer + j], tiles[i, a]) * scales[i, a]
                sums[i] += dot_nt(into[1, i * outer + j], tiles[i, b]) * scales[i, b]
        return sums

    for copy in ask:
        copy.start()
    send_own(x_panel, x_send, x_recv)
    pass_on(x_panel, x_send, x_recv)
    for copy in ask:
        copy.wait()
    all_in(x_panel, x_send, x_recv)
    pick(crossed(x_panel), x_out)
    x_across = exchange(x_out, x_in, 0)
    for copy in x_across:
        copy.start()
    for d in range(1, side):
        for copy in p_first(d):
            copy.start()
    for copy in load_tiles:
        copy.wait()
    sums = mix_inner(crossed(x_panel))
    for d in range(1, side):
        for copy in p_first(d):
            copy.wait()
    for d in range(1, side):
        for copy in p_second(d):
            copy.start()
    for copy in x_across:
        copy.wait()
    sums = mix_outer(sums, x_in)
    for i in range(rows_here):
        s_panel[i, me_x, me_y] = sums[i].astype(BF16)
        s_ref[:, i * width : (i + 1) * width] = sums[i]
    send_own(s_panel, s_send, s_recv)

    basis = jnp.concatenate([x_ref[...], s_ref[...], p_ref[...]], axis=0)
    partial[0 : 3 * k, 0 : 3 * k] = dot_nt(basis, basis, HIGH)
    partial[0 : 3 * k, 3 * k :] = jnp.zeros((3 * k, k), F32)
    partial[3 * k :, 3 * k :] = jnp.zeros((k, k), F32)

    def chunk_out(d):
        to = lax.rem(me_b + d, n_blk)
        src = partial.at[pl.ds(pl.multiple_of(to * 8, 8), 8)]
        return to, remote(src, rs_buf.at[me_b], rs_send.at[d], rs_recv.at[d], me_g, to)

    def rs_start(d):
        to, copy = chunk_out(d)

        @pl.when(to < n_early)
        def _():
            copy.start()

    def rs_start_late(d):
        to, copy = chunk_out(d)

        @pl.when(to >= n_early)
        def _():
            copy.start()

    def add_up(buf, count):
        total = buf[0]
        for i in range(1, count):
            total += buf[i]
        return total

    def across(d):
        own = ar_buf.at[me_g]
        return remote(own, own, ar_send.at[d], ar_recv.at[d], lax.rem(me_g + d, n_grp), me_b)

    def cluster_sum():
        rs_buf[me_b] = partial[pl.ds(pl.multiple_of(me_b * 8, 8), 8)]
        each(n_blk, lambda d: chunk_out(d)[1].wait_recv())
        ar_buf[me_g] = add_up(rs_buf, n_blk)
        each(n_grp, lambda d: across(d).start())

    def rows_of(b):
        return gram_ref.at[pl.ds(pl.multiple_of(b * 8, 8), 8)]

    def chunk_back(d, who):
        return remote(
            rows_of(who), rows_of(who), ag_send.at[d], ag_recv.at[d], me_g, lax.rem(me_b + d, n_blk)
        )

    def whole_sum():
        each(n_grp, lambda d: across(d).wait())
        gram_ref[pl.ds(pl.multiple_of(me_b * 8, 8), 8)] = add_up(ar_buf, n_grp)
        each(n_blk, lambda d: chunk_back(d, me_b).start())

    each(n_blk, rs_start)

    for d in range(1, side):
        for copy in p_second(d):
            copy.wait()
    pick(crossed(p_panel), p_out)
    p_across = exchange(p_out, p_in, 2)
    start(p_across)
    pass_on(s_panel, s_send, s_recv)
    sums = mix_inner(crossed(p_panel))
    wait(p_across)
    u = jnp.concatenate(mix_outer(sums, p_in), axis=1)
    partial[3 * k :, 0 : 3 * k] = dot_nt(u, basis, HIGH)
    each(n_blk, rs_start_late)

    @pl.when(me_b < n_early)
    def _():
        cluster_sum()

    all_in(s_panel, s_send, s_recv)
    pick(crossed(s_panel), s_out)
    s_across = exchange(s_out, s_in, 4)
    start(s_across)
    sums = mix_inner(crossed(s_panel))
    wait(s_across)
    t = jnp.concatenate(mix_outer(sums, s_in), axis=1)
    mine_t[:, 0 : 3 * k] = dot_nt(t, basis, HIGH)
    mine_t[:, 3 * k :] = jnp.zeros((k, k), F32)

    def half_of(ref, c):
        return ref.at[pl.ds(pl.multiple_of(c * half, 8), half)]

    to_mate = remote(half_of(mine_t, 1 - core), mate_t, mate_send.at[0], mate_recv.at[0], mate, me_b)
    to_mate.start()

    @pl.when(me_b >= n_early)
    def _():
        cluster_sum()

    to_mate.wait()
    blk_t[me_b] = mine_t[pl.ds(pl.multiple_of(core * half, 8), half)] + mate_t[...]

    def t_blk(d):
        own = blk_t.at[me_b]
        return remote(own, own, blk_send.at[d], blk_recv.at[d], me_g, lax.rem(me_b + d, n_blk))

    each(n_blk, lambda d: t_blk(d).start())

    @pl.when(me_b < n_early)
    def _():
        whole_sum()

    each(n_blk, lambda d: t_blk(d).wait())
    z_t[me_g // 2] = add_up(blk_t, n_blk)

    def t_z(d):
        own = z_t.at[me_g // 2]
        return remote(own, own, zt_send.at[d], zt_recv.at[d], lax.rem(me_g + 2 * d, n_grp), me_b)

    each(n_grp // 2, lambda d: t_z(d).start())

    @pl.when(me_b >= n_early)
    def _():
        whole_sum()

    each(n_grp // 2, lambda d: t_z(d).wait())
    image_ref[pl.ds(pl.multiple_of(core * half, 8), half)] = add_up(z_t, n_grp // 2)
    own_half = half_of(image_ref, core)
    back = remote(own_half, own_half, mate_send.at[1], mate_recv.at[1], mate, me_b)
    back.start()
    each(n_blk, lambda d: chunk_back(d, lax.rem(me_b + n_blk - d, n_blk)).wait_recv())
    each(n_blk, lambda d: chunk_back(d, me_b).wait_send())
    each(n_blk, lambda d: chunk_out(d)[1].wait_send())
    back.wait()


def first_kernel(mesh, tiles, cols, scales, x, p):
    n_grp, n_blk = mesh.shape["grp"], mesh.shape["blk"]
    side = 4
    k, here = x.shape
    rows_here, slots, width, _ = tiles.shape
    outer = rows_here * (slots // 8)
    vmem = pl.BlockSpec(memory_space=pltpu.VMEM)
    hbm = pl.BlockSpec(memory_space=pl.ANY)
    dma = pltpu.SemaphoreType.DMA
    across = pltpu.VMEM((2, outer, k, width), BF16)
    panel = pltpu.VMEM((rows_here, side, side, k, width), BF16)
    return pl.pallas_call(
        functools.partial(collect, n_grp, n_blk, side),
        out_shape=(
            jax.ShapeDtypeStruct((4 * k, 4 * k), F32),
            jax.ShapeDtypeStruct((k, 4 * k), F32),
            jax.ShapeDtypeStruct((k, here), F32),
        ),
        in_specs=[hbm] * 5,
        out_specs=(vmem, vmem, vmem),
        scratch_shapes=[
            pltpu.SMEM(cols.shape, jnp.int32),
            pltpu.SMEM(cols.shape, F32),
            pltpu.VMEM(x.shape, F32),
            pltpu.VMEM(x.shape, F32),
            pltpu.VMEM(tiles.shape, BF16),
            panel,
            panel,
            panel,
            pltpu.SMEM(cols.shape, jnp.int32),
            pltpu.SMEM(cols.shape, jnp.int32),
            across,
            across,
            across,
            across,
            across,
            across,
            pltpu.VMEM((4 * k, 4 * k), F32),
            pltpu.VMEM((n_blk, 8, 4 * k), F32),
            pltpu.VMEM((n_grp, 8, 4 * k), F32),
            pltpu.VMEM((k, 4 * k), F32),
            pltpu.VMEM((k // 2, 4 * k), F32),
            pltpu.VMEM((n_blk, k // 2, 4 * k), F32),
            pltpu.VMEM((n_grp // 2, k // 2, 4 * k), F32),
            dma((4 + rows_here,)),
            dma((2,)),
            dma((2,)),
            dma((2, side + 1, side)),
            dma((2, side + 1, side)),
            dma((2, side)),
            dma((2, side)),
            dma((2, side)),
            dma((2, side)),
            dma((2, side + 1, side)),
            dma((2, side + 1, side)),
            dma((6,)),
            dma((6,)),
            dma((n_blk,)),
            dma((n_blk,)),
            dma((n_grp,)),
            dma((n_grp,)),
            dma((n_blk,)),
            dma((n_blk,)),
            dma((2,)),
            dma((2,)),
            dma((n_blk,)),
            dma((n_blk,)),
            dma((n_grp // 2,)),
            dma((n_grp // 2,)),
        ],
        compiler_params=pltpu.CompilerParams(
            collective_id=0, has_side_effects=True, vmem_limit_bytes=56 * 2**20
        ),
        name="spread_and_mix",
    )(cols, scales, x, p, tiles)


def column(a, j, lanes):
    return jnp.broadcast_to(a[:, j : j + 1], (a.shape[0], lanes))


def spread_row(a, r):
    return jnp.broadcast_to(a[r : r + 1], a.shape)


def combine(
    inv_count, gram_ref, image_ref, s_ref, x_hbm, p_hbm, xn_ref, pn_ref, x_ref, p_ref, load_sem
):
    load = [
        pltpu.make_async_copy(x_hbm, x_ref, load_sem.at[0]),
        pltpu.make_async_copy(p_hbm, p_ref, load_sem.at[1]),
    ]
    for copy in load:
        copy.start()
    k = x_ref.shape[0]
    n = 3 * k
    gram = gram_ref[...] * inv_count
    on_t = (image_ref[...] * inv_count)[:, :n]
    basis = gram[:n, :n]
    raw = jnp.concatenate([basis[:, k : 2 * k], on_t.T, gram[n:, :n].T], axis=1)
    images = 0.5 * (raw + raw.T)

    groups = n // 8
    left = [basis[8 * q : 8 * q + 8] for q in range(groups)]
    right = [images[8 * q : 8 * q + 8] for q in range(groups)]
    pivots = [None] * groups
    coupling = None
    sub = lax.broadcasted_iota(jnp.int32, (8, n), 0)
    for start in range(0, n, PANEL):
        panel = [
            [column(left[g], start + c, n) for g in range(groups)] for c in range(PANEL)
        ]
        for c in range(PANEL):
            j = start + c
            q, r = j // 8, j % 8
            inv = 1.0 / spread_row(panel[c][q], r)
            pivots[q] = inv if r == 0 else jnp.where(sub == r, inv, pivots[q])
            here = [
                jnp.where(sub == r, 0.0, panel[c][g]) if g == q else panel[c][g]
                for g in range(groups)
            ]
            for later in range(c + 1, PANEL):
                factor = spread_row(panel[later][q], r) * inv
                panel[later] = [panel[later][g] - here[g] * factor for g in range(groups)]
            row_left = spread_row(left[q], r) * inv
            row_right = spread_row(right[q], r) * inv
            left = [left[g] - here[g] * row_left for g in range(groups)]
            right = [right[g] - here[g] * row_right for g in range(groups)]
            if j == k - 1:
                coupling = jnp.concatenate(
                    [(left[g] * pivots[g])[:, k : 2 * k] for g in range(k // 8)], axis=0
                )
    operator = jnp.concatenate([right[g] * pivots[g] for g in range(groups)], axis=0)

    here = lax.broadcasted_iota(jnp.int32, (n, n), 0) == lax.broadcasted_iota(jnp.int32, (n, n), 1)
    shift = jnp.sum(jnp.where(here, operator, 0.0), keepdims=True) * (1.0 / n)
    centred = operator - jnp.where(here, jnp.broadcast_to(shift, (n, n)), 0.0)
    size = jnp.sum(centred * centred.T, keepdims=True)
    iterate = centred * jnp.broadcast_to(lax.rsqrt(size + 1e-6), (n, n))
    for _ in range(NS_STEPS - 1):
        iterate = 1.5 * iterate - 0.5 * dot_nn(iterate, dot_nn(iterate, iterate))
    first = iterate[:, :k]
    first = 1.5 * first - 0.5 * dot_nn(iterate, dot_nn(iterate, first))
    coefficients = 0.5 * (jnp.where(here[:, :k], 1.0, 0.0) + first)

    flat = coefficients.T
    gram_new = dot_nn(flat, dot_nn(basis, coefficients))
    both = jnp.concatenate([gram_new, flat], axis=1)
    lanes = both.shape[1]
    rows = [both[8 * q : 8 * q + 8] for q in range(k // 8)]
    sub = lax.broadcasted_iota(jnp.int32, (8, lanes), 0)
    scale = [None] * (k // 8)
    for start in range(0, k, PANEL):
        first = start // 8
        below = range(first, k // 8)
        panel = [{g: column(rows[g], start + c, lanes) for g in below} for c in range(PANEL)]
        for c in range(PANEL):
            q, r = (start + c) // 8, (start + c) % 8
            pivot = spread_row(panel[c][q], r)
            inv = 1.0 / pivot
            root = lax.rsqrt(pivot)
            scale[q] = root if r == 0 else jnp.where(sub == r, root, scale[q])
            here = {
                g: jnp.where(sub <= r, 0.0, panel[c][g]) if g == q else panel[c][g] for g in below
            }
            for later in range(c + 1, PANEL):
                factor = spread_row(panel[later][q], r) * inv
                panel[later] = {g: panel[later][g] - here[g] * factor for g in below}
            row = spread_row(rows[q], r) * inv
            for g in below:
                rows[g] = rows[g] - here[g] * row
    solved = jnp.concatenate([rows[g] * scale[g] for g in range(k // 8)], axis=0)[:, k:]

    on_residual = solved[:, k : 2 * k]
    back = dot_nt(on_residual, coupling, HIGH)
    weights = jnp.concatenate(
        [solved, jnp.concatenate([-back, solved[:, k:]], axis=1)], axis=0
    )
    for copy in load:
        copy.wait()
    out = (
        dot_nn(weights[:, :k], x_ref[...])
        + dot_nn(weights[:, k : 2 * k], s_ref[...])
        + dot_nn(weights[:, 2 * k :], p_ref[...])
    )
    xn_ref[...] = out[:k]
    pn_ref[...] = out[k:]


def second_kernel(items, gram, image, s, x, p):
    vmem = pl.BlockSpec(memory_space=pltpu.VMEM)
    hbm = pl.BlockSpec(memory_space=pl.ANY)
    return pl.pallas_call(
        functools.partial(combine, 1.0 / items),
        out_shape=(
            jax.ShapeDtypeStruct(x.shape, F32),
            jax.ShapeDtypeStruct(p.shape, F32),
        ),
        in_specs=[vmem, vmem, vmem, hbm, hbm],
        out_specs=(vmem, vmem),
        scratch_shapes=[
            pltpu.VMEM(x.shape, F32),
            pltpu.VMEM(p.shape, F32),
            pltpu.SemaphoreType.DMA((2,)),
        ],
        compiler_params=pltpu.CompilerParams(vmem_limit_bytes=56 * 2**20),
        name="rayleigh_ritz",
    )(gram, image, s, x, p)


def solution(mesh):
    def per_device(tiles, cols, scales, x, p):
        items = x.shape[1] * mesh.shape["grp"] * mesh.shape["blk"]
        gram, image, s = first_kernel(mesh, tiles, cols, scales, x, p)
        return second_kernel(items, gram, image, s, x, p)

    placed = (
        P(("grp", "blk"), None, None, None),
        P(("grp", "blk"), None),
        P(("grp", "blk"), None),
        P(None, ("grp", "blk")),
        P(None, ("grp", "blk")),
    )
    return jax.shard_map(
        per_device,
        mesh=mesh,
        in_specs=placed,
        out_specs=(P(None, ("grp", "blk")), P(None, ("grp", "blk"))),
        check_vma=False,
    )
```

```python
import functools

import jax
import jax.numpy as jnp
from jax import lax
from jax.experimental import pallas as pl
from jax.experimental.pallas import tpu as pltpu
from jax.sharding import PartitionSpec as P

NS_STEPS = 8
PANEL = 8
HIGH = lax.Precision.HIGHEST
F32 = jnp.float32
BF16 = jnp.bfloat16


def dot_nt(a, b, precision=None):
    return lax.dot_general(
        a, b, (((1,), (1,)), ((), ())), precision=precision, preferred_element_type=F32
    )


def dot_nn(a, b, precision=HIGH):
    return jnp.dot(a, b, precision=precision, preferred_element_type=F32)


def column(a, j, lanes):
    return jnp.broadcast_to(a[:, j : j + 1], (a.shape[0], lanes))


def spread_row(a, r):
    return jnp.broadcast_to(a[r : r + 1], a.shape)


def invert(gram, k):
    n, lanes = gram.shape[0], 128
    groups = n // PANEL
    sub = lax.broadcasted_iota(jnp.int32, (PANEL, lanes), 0)
    lane = lax.broadcasted_iota(jnp.int32, (PANEL, lanes), 1)
    left = [gram[PANEL * g : PANEL * g + PANEL] for g in range(groups)]
    right = [jnp.where(lane == sub + PANEL * g, 1.0, 0.0) for g in range(groups)]

    def turn(_, both):
        left, right = list(both[:groups]), list(both[groups:])
        panel = [[column(left[g], c, lanes) for g in range(groups)] for c in range(PANEL)]
        pivots = None
        for c in range(PANEL):
            inv = 1.0 / spread_row(panel[c][0], c)
            pivots = inv if c == 0 else jnp.where(sub == c, inv, pivots)
            here = [jnp.where(sub == c, 0.0, panel[c][0]), *panel[c][1:]]
            for later in range(c + 1, PANEL):
                factor = spread_row(panel[later][0], c) * inv
                panel[later] = [panel[later][g] - here[g] * factor for g in range(groups)]
            row_left = spread_row(left[0], c) * inv
            row_right = spread_row(right[0], c) * inv
            left = [left[g] - here[g] * row_left for g in range(groups)]
            right = [right[g] - here[g] * row_right for g in range(groups)]
        left[0], right[0] = left[0] * pivots, right[0] * pivots
        left = [pltpu.roll(a, lanes - PANEL, 1) for a in left]
        return (*left[1:], left[0], *right[1:], right[0])

    turns = k // PANEL
    both = lax.fori_loop(0, turns, turn, (*left, *right))
    coupling = jnp.concatenate(both[groups - turns : groups], axis=0)[:, :k]
    both = lax.fori_loop(turns, groups, turn, both)
    return jnp.concatenate(both[groups:], axis=0), coupling


def collect(
    n_grp,
    n_blk,
    side,
    inv_count,
    cols_hbm,
    scales_hbm,
    x_hbm,
    p_hbm,
    tiles_hbm,
    gram_ref,
    image_ref,
    inverse_ref,
    coupling_ref,
    s_ref,
    cols,
    scales,
    x_ref,
    p_ref,
    tiles,
    x_panel,
    p_panel,
    s_panel,
    want_next,
    want_prev,
    x_out,
    x_in,
    p_out,
    p_in,
    s_out,
    s_in,
    partial,
    rs_buf,
    ar_buf,
    mine_t,
    mate_t,
    blk_t,
    z_t,
    load_sem,
    ask_send,
    ask_recv,
    x_send,
    x_recv,
    p_send,
    p_recv,
    p_send2,
    p_recv2,
    s_send,
    s_recv,
    z_send,
    z_recv,
    rs_send,
    rs_recv,
    ar_send,
    ar_recv,
    ag_send,
    ag_recv,
    mate_send,
    mate_recv,
    blk_send,
    blk_recv,
    zt_send,
    zt_recv,
):
    me_g = lax.axis_index("grp")
    me_b = lax.axis_index("blk")
    me_x, me_y = me_b // side, lax.rem(me_b, side)
    nxt = lax.rem(me_g + 1, n_grp)
    prv = lax.rem(me_g + n_grp - 1, n_grp)
    core = lax.rem(me_g, 2)
    mate = me_g + 1 - 2 * core
    rows_here, slots = cols.shape
    k = x_ref.shape[0]
    width = tiles.shape[2]
    cluster = n_blk * rows_here
    inner = 3 * slots // 4
    outer = slots // 8
    n_early = 3 * k // 8
    half = k // 2

    def load(src, dst, i):
        return pltpu.make_async_copy(src, dst, load_sem.at[i])

    load_x, load_p = load(x_hbm, x_ref, 0), load(p_hbm, p_ref, 1)
    load_small = [load(cols_hbm, cols, 2), load(scales_hbm, scales, 3)]
    load_tiles = [load(tiles_hbm.at[i], tiles.at[i], 4 + i) for i in range(rows_here)]
    load_x.start()
    barrier = pltpu.get_barrier_semaphore()

    def greet(grp, blk):
        pl.semaphore_signal(
            barrier, inc=1, device_id=(grp, blk), device_id_type=pl.DeviceIdType.MESH
        )

    def greet_blk(d, c):
        greet(me_g, lax.rem(me_b + d, n_blk))
        return c

    def greet_grp(d, c):
        greet(lax.rem(me_g + d, n_grp), me_b)
        return c

    lax.fori_loop(1, n_blk, greet_blk, 0)
    lax.fori_loop(1, n_grp, greet_grp, 0)
    for copy in [*load_small, load_p, *load_tiles]:
        copy.start()

    def block(ref, i):
        return ref[:, i * width : (i + 1) * width].astype(BF16)

    load_x.wait()
    for i in range(rows_here):
        x_panel[i, me_x, me_y] = block(x_ref, i)
    pl.semaphore_wait(barrier, n_blk - 1 + n_grp - 1)

    def remote(src, dst, send, recv, grp, blk):
        return pltpu.make_async_remote_copy(
            src_ref=src,
            dst_ref=dst,
            send_sem=send,
            recv_sem=recv,
            device_id=(grp, blk),
            device_id_type=pl.DeviceIdType.MESH,
        )

    ask = [
        remote(cols, want_next, ask_send.at[0], ask_recv.at[0], prv, me_b),
        remote(cols, want_prev, ask_send.at[1], ask_recv.at[1], nxt, me_b),
    ]

    def each(count, act):
        def body(d, c):
            act(d)
            return c

        lax.fori_loop(1, count, body, 0)

    def along_x(d):
        return lax.rem(me_x + d, side) * side + me_y

    def along_y(d):
        return me_x * side + lax.rem(me_y + d, side)

    def p_first(d):
        a, b = p_panel.at[0, me_x, me_y], p_panel.at[1, me_x, me_y]
        return [
            remote(a, a, p_send.at[0, d], p_recv.at[0, d], me_g, along_x(d)),
            remote(b, b, p_send.at[1, d], p_recv.at[1, d], me_g, along_y(d)),
        ]

    def p_second(d):
        a, b = p_panel.at[0, :, me_y], p_panel.at[1, me_x]
        return [
            remote(a, a, p_send2.at[0, d], p_recv2.at[0, d], me_g, along_y(d)),
            remote(b, b, p_send2.at[1, d], p_recv2.at[1, d], me_g, along_x(d)),
        ]

    def near(buf, send, recv, d):
        a, b = buf.at[0, me_x, me_y], buf.at[1, me_x, me_y]
        return [
            remote(a, a, send.at[0, side, d], recv.at[0, side, d], me_g, along_x(d)),
            remote(b, b, send.at[1, side, d], recv.at[1, side, d], me_g, along_y(d)),
        ]

    def onward(buf, send, recv, e, d):
        from_x, from_y = lax.rem(me_x + side - e, side), lax.rem(me_y + side - e, side)
        a, b = buf.at[0, from_x, me_y], buf.at[1, me_x, from_y]
        return [
            remote(a, a, send.at[0, e, d], recv.at[0, e, d], me_g, along_y(d)),
            remote(b, b, send.at[1, e, d], recv.at[1, e, d], me_g, along_x(d)),
        ]

    def start(copies):
        for copy in copies:
            copy.start()

    def wait(copies):
        for copy in copies:
            copy.wait()

    def send_own(buf, send, recv):
        each(side, lambda d: start(near(buf, send, recv, d)))
        each(side, lambda d: start(onward(buf, send, recv, 0, d)))

    def pass_on(buf, send, recv):
        def arrived(e):
            for copy in near(buf, send, recv, e):
                copy.wait_recv()
            each(side, lambda d: start(onward(buf, send, recv, e, d)))

        each(side, arrived)

    def all_in(buf, send, recv):
        def sent(d):
            for copy in near(buf, send, recv, d):
                copy.wait_send()
            wait(onward(buf, send, recv, 0, d))

        each(side, sent)
        each(side, lambda e: each(side, lambda d: wait(onward(buf, send, recv, e, d))))

    def crossed(buf):
        def get(c):
            c = lax.rem(c, cluster)
            at = c // rows_here
            return buf[lax.rem(c, rows_here), at // side, lax.rem(at, side)]

        return get

    def exchange(out, into, at):
        return [
            remote(out.at[0], into.at[0], z_send.at[at], z_recv.at[at], nxt, me_b),
            remote(out.at[1], into.at[1], z_send.at[at + 1], z_recv.at[at + 1], prv, me_b),
        ]

    def pick(get, out):
        for i in range(rows_here):
            for j in range(outer):
                out[0, i * outer + j] = get(want_next[i, inner + j])
                out[1, i * outer + j] = get(want_prev[i, inner + outer + j])

    def mix_inner(get):
        sums = []
        for i in range(rows_here):

            def body(j, acc, i=i):
                return acc + dot_nt(get(cols[i, j]), tiles[i, j]) * scales[i, j]

            sums.append(lax.fori_loop(0, inner, body, jnp.zeros((k, width), F32), unroll=8))
        return sums

    def mix_outer(sums, into):
        for i in range(rows_here):
            for j in range(outer):
                a, b = inner + j, inner + outer + j
                sums[i] += dot_nt(into[0, i * outer + j], tiles[i, a]) * scales[i, a]
                sums[i] += dot_nt(into[1, i * outer + j], tiles[i, b]) * scales[i, b]
        return sums

    send_own(x_panel, x_send, x_recv)
    wait(load_small)
    start(ask)
    load_p.wait()
    for i in range(rows_here):
        p_panel[i, me_x, me_y] = block(p_ref, i)
    pass_on(x_panel, x_send, x_recv)
    for d in range(1, side):
        for copy in p_first(d):
            copy.start()
    for copy in ask:
        copy.wait()
    all_in(x_panel, x_send, x_recv)
    pick(crossed(x_panel), x_out)
    x_across = exchange(x_out, x_in, 0)
    for copy in x_across:
        copy.start()
    for d in range(1, side):
        for copy in p_first(d):
            copy.wait()
    for d in range(1, side):
        for copy in p_second(d):
            copy.start()
    for copy in load_tiles:
        copy.wait()
    sums = mix_inner(crossed(x_panel))
    for copy in x_across:
        copy.wait()
    sums = mix_outer(sums, x_in)
    for i in range(rows_here):
        s_panel[i, me_x, me_y] = sums[i].astype(BF16)
        s_ref[:, i * width : (i + 1) * width] = sums[i]
    send_own(s_panel, s_send, s_recv)

    basis = jnp.concatenate([x_ref[...], s_ref[...], p_ref[...]], axis=0)
    partial[0 : 3 * k, 0 : 3 * k] = dot_nt(basis, basis, HIGH)
    partial[0 : 3 * k, 3 * k :] = jnp.zeros((3 * k, k), F32)
    partial[3 * k :, 3 * k :] = jnp.zeros((k, k), F32)

    def chunk_out(d):
        to = lax.rem(me_b + d, n_blk)
        src = partial.at[pl.ds(pl.multiple_of(to * 8, 8), 8)]
        return to, remote(src, rs_buf.at[me_b], rs_send.at[d], rs_recv.at[d], me_g, to)

    def rs_start(d):
        to, copy = chunk_out(d)

        @pl.when(to < n_early)
        def _():
            copy.start()

    def rs_start_late(d):
        to, copy = chunk_out(d)

        @pl.when(to >= n_early)
        def _():
            copy.start()

    def add_up(buf, count):
        total = buf[0]
        for i in range(1, count):
            total += buf[i]
        return total

    def across(d):
        own = ar_buf.at[me_g]
        return remote(own, own, ar_send.at[d], ar_recv.at[d], lax.rem(me_g + d, n_grp), me_b)

    def cluster_sum():
        rs_buf[me_b] = partial[pl.ds(pl.multiple_of(me_b * 8, 8), 8)]
        each(n_blk, lambda d: chunk_out(d)[1].wait_recv())
        ar_buf[me_g] = add_up(rs_buf, n_blk)
        each(n_grp, lambda d: across(d).start())

    def rows_of(b):
        return gram_ref.at[pl.ds(pl.multiple_of(b * 8, 8), 8)]

    def chunk_back(d, who):
        return remote(
            rows_of(who), rows_of(who), ag_send.at[d], ag_recv.at[d], me_g, lax.rem(me_b + d, n_blk)
        )

    def whole_sum():
        each(n_grp, lambda d: across(d).wait())
        gram_ref[pl.ds(pl.multiple_of(me_b * 8, 8), 8)] = add_up(ar_buf, n_grp)
        each(n_blk, lambda d: chunk_back(d, me_b).start())

    each(n_blk, rs_start)

    for d in range(1, side):
        for copy in p_second(d):
            copy.wait()
    pick(crossed(p_panel), p_out)
    p_across = exchange(p_out, p_in, 2)
    start(p_across)
    pass_on(s_panel, s_send, s_recv)
    sums = mix_inner(crossed(p_panel))
    wait(p_across)
    u = jnp.concatenate(mix_outer(sums, p_in), axis=1)
    partial[3 * k :, 0 : 3 * k] = dot_nt(u, basis, HIGH)
    each(n_blk, rs_start_late)
    all_in(s_panel, s_send, s_recv)
    pick(crossed(s_panel), s_out)
    s_across = exchange(s_out, s_in, 4)
    start(s_across)

    @pl.when(me_b < n_early)
    def _():
        cluster_sum()

    sums = mix_inner(crossed(s_panel))
    wait(s_across)
    t = jnp.concatenate(mix_outer(sums, s_in), axis=1)
    mine_t[:, 0 : 3 * k] = dot_nt(t, basis, HIGH)
    mine_t[:, 3 * k :] = jnp.zeros((k, k), F32)

    def half_of(ref, c):
        return ref.at[pl.ds(pl.multiple_of(c * half, 8), half)]

    to_mate = remote(half_of(mine_t, 1 - core), mate_t, mate_send.at[0], mate_recv.at[0], mate, me_b)
    to_mate.start()

    @pl.when(me_b >= n_early)
    def _():
        cluster_sum()

    to_mate.wait()
    blk_t[me_b] = mine_t[pl.ds(pl.multiple_of(core * half, 8), half)] + mate_t[...]

    def t_blk(d):
        own = blk_t.at[me_b]
        return remote(own, own, blk_send.at[d], blk_recv.at[d], me_g, lax.rem(me_b + d, n_blk))

    each(n_blk, lambda d: t_blk(d).start())

    @pl.when(me_b < n_early)
    def _():
        whole_sum()

    def back_from(early):
        def arrived(d):
            source = lax.rem(me_b + n_blk - d, n_blk)

            @pl.when((source < n_early) if early else (source >= n_early))
            def _():
                chunk_back(d, source).wait_recv()

        return arrived

    each(n_blk, lambda d: t_blk(d).wait())
    z_t[me_g // 2] = add_up(blk_t, n_blk)

    def t_z(d):
        own = z_t.at[me_g // 2]
        return remote(own, own, zt_send.at[d], zt_recv.at[d], lax.rem(me_g + 2 * d, n_grp), me_b)

    each(n_grp // 2, lambda d: t_z(d).start())

    @pl.when(me_b >= n_early)
    def _():
        whole_sum()

    each(n_blk, back_from(True))
    inverse, coupling = invert(gram_ref[0 : 3 * k] * inv_count, k)
    inverse_ref[...] = inverse
    coupling_ref[...] = coupling
    each(n_grp // 2, lambda d: t_z(d).wait())
    image_ref[pl.ds(pl.multiple_of(core * half, 8), half)] = add_up(z_t, n_grp // 2)
    own_half = half_of(image_ref, core)
    back = remote(own_half, own_half, mate_send.at[1], mate_recv.at[1], mate, me_b)
    back.start()
    each(n_blk, back_from(False))
    each(n_blk, lambda d: chunk_back(d, me_b).wait_send())
    each(n_blk, lambda d: chunk_out(d)[1].wait_send())
    back.wait()


def first_kernel(mesh, items, tiles, cols, scales, x, p):
    n_grp, n_blk = mesh.shape["grp"], mesh.shape["blk"]
    side = 4
    k, here = x.shape
    rows_here, slots, width, _ = tiles.shape
    outer = rows_here * (slots // 8)
    vmem = pl.BlockSpec(memory_space=pltpu.VMEM)
    hbm = pl.BlockSpec(memory_space=pl.ANY)
    dma = pltpu.SemaphoreType.DMA
    across = pltpu.VMEM((2, outer, k, width), BF16)
    panel = pltpu.VMEM((rows_here, side, side, k, width), BF16)
    return pl.pallas_call(
        functools.partial(collect, n_grp, n_blk, side, 1.0 / items),
        out_shape=(
            jax.ShapeDtypeStruct((4 * k, 4 * k), F32),
            jax.ShapeDtypeStruct((k, 4 * k), F32),
            jax.ShapeDtypeStruct((3 * k, 4 * k), F32),
            jax.ShapeDtypeStruct((k, k), F32),
            jax.ShapeDtypeStruct((k, here), F32),
        ),
        in_specs=[hbm] * 5,
        out_specs=(vmem,) * 5,
        scratch_shapes=[
            pltpu.SMEM(cols.shape, jnp.int32),
            pltpu.SMEM(cols.shape, F32),
            pltpu.VMEM(x.shape, F32),
            pltpu.VMEM(x.shape, F32),
            pltpu.VMEM(tiles.shape, BF16),
            panel,
            panel,
            panel,
            pltpu.SMEM(cols.shape, jnp.int32),
            pltpu.SMEM(cols.shape, jnp.int32),
            across,
            across,
            across,
            across,
            across,
            across,
            pltpu.VMEM((4 * k, 4 * k), F32),
            pltpu.VMEM((n_blk, 8, 4 * k), F32),
            pltpu.VMEM((n_grp, 8, 4 * k), F32),
            pltpu.VMEM((k, 4 * k), F32),
            pltpu.VMEM((k // 2, 4 * k), F32),
            pltpu.VMEM((n_blk, k // 2, 4 * k), F32),
            pltpu.VMEM((n_grp // 2, k // 2, 4 * k), F32),
            dma((4 + rows_here,)),
            dma((2,)),
            dma((2,)),
            dma((2, side + 1, side)),
            dma((2, side + 1, side)),
            dma((2, side)),
            dma((2, side)),
            dma((2, side)),
            dma((2, side)),
            dma((2, side + 1, side)),
            dma((2, side + 1, side)),
            dma((6,)),
            dma((6,)),
            dma((n_blk,)),
            dma((n_blk,)),
            dma((n_grp,)),
            dma((n_grp,)),
            dma((n_blk,)),
            dma((n_blk,)),
            dma((2,)),
            dma((2,)),
            dma((n_blk,)),
            dma((n_blk,)),
            dma((n_grp // 2,)),
            dma((n_grp // 2,)),
        ],
        compiler_params=pltpu.CompilerParams(
            collective_id=0, has_side_effects=True, vmem_limit_bytes=56 * 2**20
        ),
        name="spread_and_mix",
    )(cols, scales, x, p, tiles)


def combine(
    inv_count,
    gram_ref,
    image_ref,
    inverse_ref,
    coupling_ref,
    s_ref,
    x_hbm,
    p_hbm,
    xn_ref,
    pn_ref,
    rows_ref,
    load_sem,
):
    k = s_ref.shape[0]
    n = 3 * k
    load = [
        pltpu.make_async_copy(x_hbm, rows_ref.at[0:k], load_sem.at[0]),
        pltpu.make_async_copy(p_hbm, rows_ref.at[2 * k : n], load_sem.at[1]),
    ]
    for copy in load:
        copy.start()
    rows_ref[k : 2 * k] = s_ref[...]
    gram = gram_ref[...] * inv_count
    on_t = (image_ref[...] * inv_count)[:, :n]
    basis = gram[:n, :n]
    raw = jnp.concatenate([basis[:, k : 2 * k], on_t.T, gram[n:, :n].T], axis=1)
    images = 0.5 * (raw + raw.T)

    operator = dot_nn(inverse_ref[:, :n], images)

    here = lax.broadcasted_iota(jnp.int32, (n, n), 0) == lax.broadcasted_iota(jnp.int32, (n, n), 1)
    shift = jnp.sum(jnp.where(here, operator, 0.0), keepdims=True) * (1.0 / n)
    centred = operator - jnp.where(here, jnp.broadcast_to(shift, (n, n)), 0.0)
    size = jnp.sum(centred * centred.T, keepdims=True)
    iterate = centred * jnp.broadcast_to(lax.rsqrt(size + 1e-6), (n, n))
    for _ in range(NS_STEPS - 1):
        iterate = 1.5 * iterate - 0.5 * dot_nn(iterate, dot_nn(iterate, iterate))
    first = iterate[:, :k]
    first = 1.5 * first - 0.5 * dot_nn(iterate, dot_nn(iterate, first))
    coefficients = 0.5 * (jnp.where(here[:, :k], 1.0, 0.0) + first)

    flat = coefficients.T
    gram_new = dot_nn(flat, dot_nn(basis, coefficients))
    both = jnp.concatenate([gram_new, flat], axis=1)
    lanes = both.shape[1]
    rows = [both[8 * q : 8 * q + 8] for q in range(k // 8)]
    sub = lax.broadcasted_iota(jnp.int32, (8, lanes), 0)
    scale = [None] * (k // 8)
    for start in range(0, k, PANEL):
        first = start // 8
        below = range(first, k // 8)
        panel = [{g: column(rows[g], start + c, lanes) for g in below} for c in range(PANEL)]
        for c in range(PANEL):
            q, r = (start + c) // 8, (start + c) % 8
            pivot = spread_row(panel[c][q], r)
            inv = 1.0 / pivot
            root = lax.rsqrt(pivot)
            scale[q] = root if r == 0 else jnp.where(sub == r, root, scale[q])
            here = {
                g: jnp.where(sub <= r, 0.0, panel[c][g]) if g == q else panel[c][g] for g in below
            }
            for later in range(c + 1, PANEL):
                factor = spread_row(panel[later][q], r) * inv
                panel[later] = {g: panel[later][g] - here[g] * factor for g in below}
            row = spread_row(rows[q], r) * inv
            for g in below:
                rows[g] = rows[g] - here[g] * row
    solved = jnp.concatenate([rows[g] * scale[g] for g in range(k // 8)], axis=0)[:, k:]

    on_residual = solved[:, k : 2 * k]
    back = dot_nt(on_residual, coupling_ref[...], HIGH)
    weights = jnp.concatenate(
        [solved, jnp.concatenate([-back, solved[:, k:]], axis=1)], axis=0
    )
    for copy in load:
        copy.wait()
    out = dot_nn(weights, rows_ref[...])
    xn_ref[...] = out[:k]
    pn_ref[...] = out[k:]


def second_kernel(items, gram, image, inverse, coupling, s, x, p):
    vmem = pl.BlockSpec(memory_space=pltpu.VMEM)
    hbm = pl.BlockSpec(memory_space=pl.ANY)
    return pl.pallas_call(
        functools.partial(combine, 1.0 / items),
        out_shape=(
            jax.ShapeDtypeStruct(x.shape, F32),
            jax.ShapeDtypeStruct(p.shape, F32),
        ),
        in_specs=[vmem] * 5 + [hbm] * 2,
        out_specs=(vmem, vmem),
        scratch_shapes=[
            pltpu.VMEM((3 * x.shape[0], x.shape[1]), F32),
            pltpu.SemaphoreType.DMA((2,)),
        ],
        compiler_params=pltpu.CompilerParams(vmem_limit_bytes=56 * 2**20),
        name="rayleigh_ritz",
    )(gram, image, inverse, coupling, s, x, p)


def solution(mesh):
    def per_device(tiles, cols, scales, x, p):
        items = x.shape[1] * mesh.shape["grp"] * mesh.shape["blk"]
        sums = first_kernel(mesh, items, tiles, cols, scales, x, p)
        return second_kernel(items, *sums, x, p)

    placed = (
        P(("grp", "blk"), None, None, None),
        P(("grp", "blk"), None),
        P(("grp", "blk"), None),
        P(None, ("grp", "blk")),
        P(None, ("grp", "blk")),
    )
    return jax.shard_map(
        per_device,
        mesh=mesh,
        in_specs=placed,
        out_specs=(P(None, ("grp", "blk")), P(None, ("grp", "blk"))),
        check_vma=False,
    )
```

```python
import functools

import jax
import jax.numpy as jnp
from jax import lax
from jax.experimental import pallas as pl
from jax.experimental.pallas import tpu as pltpu
from jax.sharding import PartitionSpec as P

NS_STEPS = 8
PANEL = 8
HIGH = lax.Precision.HIGHEST
F32 = jnp.float32
BF16 = jnp.bfloat16


def dot_nt(a, b, precision=None):
    return lax.dot_general(
        a, b, (((1,), (1,)), ((), ())), precision=precision, preferred_element_type=F32
    )


def dot_nn(a, b, precision=HIGH):
    return jnp.dot(a, b, precision=precision, preferred_element_type=F32)


def column(a, j, lanes):
    return jnp.broadcast_to(a[:, j : j + 1], (a.shape[0], lanes))


def spread_row(a, r):
    return jnp.broadcast_to(a[r : r + 1], a.shape)


def invert(gram, k):
    n, lanes = gram.shape[0], 128
    groups = n // PANEL
    sub = lax.broadcasted_iota(jnp.int32, (PANEL, lanes), 0)
    lane = lax.broadcasted_iota(jnp.int32, (PANEL, lanes), 1)
    left = [gram[PANEL * g : PANEL * g + PANEL] for g in range(groups)]
    right = [jnp.where(lane == sub + PANEL * g, 1.0, 0.0) for g in range(groups)]

    def turn(_, both):
        left, right = list(both[:groups]), list(both[groups:])
        panel = [[column(left[g], c, lanes) for g in range(groups)] for c in range(PANEL)]
        pivots = None
        for c in range(PANEL):
            inv = 1.0 / spread_row(panel[c][0], c)
            pivots = inv if c == 0 else jnp.where(sub == c, inv, pivots)
            here = [jnp.where(sub == c, 0.0, panel[c][0]), *panel[c][1:]]
            for later in range(c + 1, PANEL):
                factor = spread_row(panel[later][0], c) * inv
                panel[later] = [panel[later][g] - here[g] * factor for g in range(groups)]
            row_left = spread_row(left[0], c) * inv
            row_right = spread_row(right[0], c) * inv
            left = [left[g] - here[g] * row_left for g in range(groups)]
            right = [right[g] - here[g] * row_right for g in range(groups)]
        left[0], right[0] = left[0] * pivots, right[0] * pivots
        left = [pltpu.roll(a, lanes - PANEL, 1) for a in left]
        return (*left[1:], left[0], *right[1:], right[0])

    turns = k // PANEL
    both = lax.fori_loop(0, turns, turn, (*left, *right))
    coupling = jnp.concatenate(both[groups - turns : groups], axis=0)[:, :k]
    both = lax.fori_loop(turns, groups, turn, both)
    return jnp.concatenate(both[groups:], axis=0), coupling


def collect(
    n_grp,
    n_blk,
    side,
    inv_count,
    cols_hbm,
    scales_hbm,
    x_hbm,
    p_hbm,
    tiles_hbm,
    gram_ref,
    image_ref,
    inverse_ref,
    coupling_ref,
    s_ref,
    cols,
    scales,
    x_ref,
    p_ref,
    tiles,
    x_panel,
    p_panel,
    s_panel,
    wanted,
    x_out,
    x_in,
    p_out,
    p_in,
    s_out,
    s_in,
    partial,
    rs_buf,
    ar_buf,
    mine_t,
    mate_t,
    blk_t,
    z_t,
    load_sem,
    ask_send,
    ask_recv,
    x_send,
    x_recv,
    p_send,
    p_recv,
    p_send2,
    p_recv2,
    s_send,
    s_recv,
    z_send,
    z_recv,
    rs_send,
    rs_recv,
    ar_send,
    ar_recv,
    ag_send,
    ag_recv,
    mate_send,
    mate_recv,
    blk_send,
    blk_recv,
    zt_send,
    zt_recv,
):
    me_g = lax.axis_index("grp")
    me_b = lax.axis_index("blk")
    me_x, me_y = me_b // side, lax.rem(me_b, side)
    nxt = lax.rem(me_g + 1, n_grp)
    prv = lax.rem(me_g + n_grp - 1, n_grp)
    core = lax.rem(me_g, 2)
    mate = me_g + 1 - 2 * core
    rows_here, slots = cols.shape
    k = x_ref.shape[0]
    width = tiles.shape[2]
    cluster = n_blk * rows_here
    inner = 3 * slots // 4
    outer = slots // 8
    n_early = 3 * k // 8
    half = k // 2

    def load(src, dst, i):
        return pltpu.make_async_copy(src, dst, load_sem.at[i])

    load_x, load_p = load(x_hbm, x_ref, 0), load(p_hbm, p_ref, 1)
    load_small = [load(cols_hbm, cols, 2), load(scales_hbm, scales, 3)]
    load_tiles = [load(tiles_hbm.at[i], tiles.at[i], 4 + i) for i in range(rows_here)]
    load_x.start()
    barrier = pltpu.get_barrier_semaphore()

    def greet(grp, blk):
        pl.semaphore_signal(
            barrier, inc=1, device_id=(grp, blk), device_id_type=pl.DeviceIdType.MESH
        )

    def greet_blk(d, c):
        greet(me_g, lax.rem(me_b + d, n_blk))
        return c

    def greet_grp(d, c):
        greet(lax.rem(me_g + d, n_grp), me_b)
        return c

    lax.fori_loop(1, n_blk, greet_blk, 0)
    lax.fori_loop(1, n_grp, greet_grp, 0)
    for copy in [*load_small, load_p, *load_tiles]:
        copy.start()

    def block(ref, i):
        return ref[:, i * width : (i + 1) * width].astype(BF16)

    load_x.wait()
    for i in range(rows_here):
        x_panel[i, me_x, me_y] = block(x_ref, i)
    pl.semaphore_wait(barrier, n_blk - 1 + n_grp - 1)

    def remote(src, dst, send, recv, grp, blk):
        return pltpu.make_async_remote_copy(
            src_ref=src,
            dst_ref=dst,
            send_sem=send,
            recv_sem=recv,
            device_id=(grp, blk),
            device_id_type=pl.DeviceIdType.MESH,
        )

    ask = [
        remote(cols, wanted.at[0], ask_send.at[0], ask_recv.at[0], prv, me_b),
        remote(cols, wanted.at[1], ask_send.at[1], ask_recv.at[1], nxt, me_b),
    ]

    def each(count, act):
        def body(d, c):
            act(d)
            return c

        lax.fori_loop(1, count, body, 0)

    def along_x(d):
        return lax.rem(me_x + d, side) * side + me_y

    def along_y(d):
        return me_x * side + lax.rem(me_y + d, side)

    def p_first(d):
        a, b = p_panel.at[0, me_x, me_y], p_panel.at[1, me_x, me_y]
        return [
            remote(a, a, p_send.at[0, d], p_recv.at[0, d], me_g, along_x(d)),
            remote(b, b, p_send.at[1, d], p_recv.at[1, d], me_g, along_y(d)),
        ]

    def p_second(d):
        a, b = p_panel.at[0, :, me_y], p_panel.at[1, me_x]
        return [
            remote(a, a, p_send2.at[0, d], p_recv2.at[0, d], me_g, along_y(d)),
            remote(b, b, p_send2.at[1, d], p_recv2.at[1, d], me_g, along_x(d)),
        ]

    def near(buf, send, recv, d):
        a, b = buf.at[0, me_x, me_y], buf.at[1, me_x, me_y]
        return [
            remote(a, a, send.at[0, side, d], recv.at[0, side, d], me_g, along_x(d)),
            remote(b, b, send.at[1, side, d], recv.at[1, side, d], me_g, along_y(d)),
        ]

    def onward(buf, send, recv, e, d):
        from_x, from_y = lax.rem(me_x + side - e, side), lax.rem(me_y + side - e, side)
        a, b = buf.at[0, from_x, me_y], buf.at[1, me_x, from_y]
        return [
            remote(a, a, send.at[0, e, d], recv.at[0, e, d], me_g, along_y(d)),
            remote(b, b, send.at[1, e, d], recv.at[1, e, d], me_g, along_x(d)),
        ]

    def start(copies):
        for copy in copies:
            copy.start()

    def wait(copies):
        for copy in copies:
            copy.wait()

    def send_own(buf, send, recv):
        each(side, lambda d: start(near(buf, send, recv, d)))
        each(side, lambda d: start(onward(buf, send, recv, 0, d)))

    def pass_on(buf, send, recv):
        def arrived(e):
            for copy in near(buf, send, recv, e):
                copy.wait_recv()
            each(side, lambda d: start(onward(buf, send, recv, e, d)))

        each(side, arrived)

    def all_in(buf, send, recv):
        def sent(d):
            for copy in near(buf, send, recv, d):
                copy.wait_send()
            wait(onward(buf, send, recv, 0, d))

        each(side, sent)
        each(side, lambda e: each(side, lambda d: wait(onward(buf, send, recv, e, d))))

    def crossed(buf):
        def get(c):
            c = lax.rem(c, cluster)
            at = c // rows_here
            return buf[lax.rem(c, rows_here), at // side, lax.rem(at, side)]

        return get

    away = 1 - core

    def exchange(out, into, at, side):
        return remote(
            out.at[side],
            into.at[side],
            z_send.at[at + side],
            z_recv.at[at + side],
            jnp.where(side == 0, nxt, prv),
            me_b,
        )

    def hand_over(get, out, into, at):
        copies = [exchange(out, into, at, side) for side in (away, 1 - away)]
        for side, copy in zip((away, 1 - away), copies):
            for i in range(rows_here):
                for j in range(outer):
                    slot = inner + side * outer + j
                    out[side, i * outer + j] = get(wanted[side, i, slot])
            copy.start()
        return copies

    def mix_inner(get):
        sums = []
        for i in range(rows_here):

            def body(j, acc, i=i):
                return acc + dot_nt(get(cols[i, j]), tiles[i, j]) * scales[i, j]

            sums.append(lax.fori_loop(0, inner, body, jnp.zeros((k, width), F32), unroll=24))
        return sums

    def mix_outer(sums, into):
        for i in range(rows_here):
            for j in range(outer):
                a, b = inner + j, inner + outer + j
                sums[i] += dot_nt(into[0, i * outer + j], tiles[i, a]) * scales[i, a]
                sums[i] += dot_nt(into[1, i * outer + j], tiles[i, b]) * scales[i, b]
        return sums

    send_own(x_panel, x_send, x_recv)
    wait(load_small)
    start(ask)
    load_p.wait()
    for i in range(rows_here):
        p_panel[i, me_x, me_y] = block(p_ref, i)
    pass_on(x_panel, x_send, x_recv)
    for d in range(1, side):
        for copy in p_first(d):
            copy.start()
    for copy in ask:
        copy.wait()
    all_in(x_panel, x_send, x_recv)
    x_across = hand_over(crossed(x_panel), x_out, x_in, 0)
    for d in range(1, side):
        for copy in p_first(d):
            copy.wait()
    for d in range(1, side):
        for copy in p_second(d):
            copy.start()
    for copy in load_tiles:
        copy.wait()
    sums = mix_inner(crossed(x_panel))
    for copy in x_across:
        copy.wait()
    sums = mix_outer(sums, x_in)
    for i in range(rows_here):
        s_panel[i, me_x, me_y] = sums[i].astype(BF16)
        s_ref[:, i * width : (i + 1) * width] = sums[i]
    send_own(s_panel, s_send, s_recv)

    basis = jnp.concatenate([x_ref[...], s_ref[...], p_ref[...]], axis=0)
    partial[0 : 3 * k, 0 : 3 * k] = dot_nt(basis, basis, HIGH)
    partial[0 : 3 * k, 3 * k :] = jnp.zeros((3 * k, k), F32)
    partial[3 * k :, 3 * k :] = jnp.zeros((k, k), F32)

    def chunk_out(d):
        to = lax.rem(me_b + d, n_blk)
        src = partial.at[pl.ds(pl.multiple_of(to * 8, 8), 8)]
        return to, remote(src, rs_buf.at[me_b], rs_send.at[d], rs_recv.at[d], me_g, to)

    def rs_start(d):
        to, copy = chunk_out(d)

        @pl.when(to < n_early)
        def _():
            copy.start()

    def rs_start_late(d):
        to, copy = chunk_out(d)

        @pl.when(to >= n_early)
        def _():
            copy.start()

    def add_up(buf, count):
        total = buf[0]
        for i in range(1, count):
            total += buf[i]
        return total

    def across(d):
        own = ar_buf.at[me_g]
        return remote(own, own, ar_send.at[d], ar_recv.at[d], lax.rem(me_g + d, n_grp), me_b)

    def cluster_sum():
        rs_buf[me_b] = partial[pl.ds(pl.multiple_of(me_b * 8, 8), 8)]
        each(n_blk, lambda d: chunk_out(d)[1].wait_recv())
        ar_buf[me_g] = add_up(rs_buf, n_blk)
        each(n_grp, lambda d: across(d).start())

    def rows_of(b):
        return gram_ref.at[pl.ds(pl.multiple_of(b * 8, 8), 8)]

    def chunk_back(d, who):
        return remote(
            rows_of(who), rows_of(who), ag_send.at[d], ag_recv.at[d], me_g, lax.rem(me_b + d, n_blk)
        )

    def whole_sum():
        each(n_grp, lambda d: across(d).wait())
        gram_ref[pl.ds(pl.multiple_of(me_b * 8, 8), 8)] = add_up(ar_buf, n_grp)
        each(n_blk, lambda d: chunk_back(d, me_b).start())

    each(n_blk, rs_start)

    for d in range(1, side):
        for copy in p_second(d):
            copy.wait()
    p_across = hand_over(crossed(p_panel), p_out, p_in, 2)
    pass_on(s_panel, s_send, s_recv)
    sums = mix_inner(crossed(p_panel))
    wait(p_across)
    u = jnp.concatenate(mix_outer(sums, p_in), axis=1)
    partial[3 * k :, 0 : 3 * k] = dot_nt(u, basis, HIGH)
    each(n_blk, rs_start_late)
    all_in(s_panel, s_send, s_recv)
    s_across = hand_over(crossed(s_panel), s_out, s_in, 4)

    @pl.when(me_b < n_early)
    def _():
        cluster_sum()

    sums = mix_inner(crossed(s_panel))
    wait(s_across)
    t = jnp.concatenate(mix_outer(sums, s_in), axis=1)
    mine_t[:, 0 : 3 * k] = dot_nt(t, basis, HIGH)
    mine_t[:, 3 * k :] = jnp.zeros((k, k), F32)

    def half_of(ref, c):
        return ref.at[pl.ds(pl.multiple_of(c * half, 8), half)]

    to_mate = remote(half_of(mine_t, 1 - core), mate_t, mate_send.at[0], mate_recv.at[0], mate, me_b)
    to_mate.start()

    @pl.when(me_b >= n_early)
    def _():
        cluster_sum()

    to_mate.wait()
    blk_t[me_b] = mine_t[pl.ds(pl.multiple_of(core * half, 8), half)] + mate_t[...]

    def t_blk(d):
        own = blk_t.at[me_b]
        return remote(own, own, blk_send.at[d], blk_recv.at[d], me_g, lax.rem(me_b + d, n_blk))

    each(n_blk, lambda d: t_blk(d).start())

    @pl.when(me_b < n_early)
    def _():
        whole_sum()

    def back_from(early):
        def arrived(d):
            source = lax.rem(me_b + n_blk - d, n_blk)

            @pl.when((source < n_early) if early else (source >= n_early))
            def _():
                chunk_back(d, source).wait_recv()

        return arrived

    each(n_blk, lambda d: t_blk(d).wait())
    z_t[me_g // 2] = add_up(blk_t, n_blk)

    def t_z(d):
        own = z_t.at[me_g // 2]
        return remote(own, own, zt_send.at[d], zt_recv.at[d], lax.rem(me_g + 2 * d, n_grp), me_b)

    each(n_grp // 2, lambda d: t_z(d).start())

    @pl.when(me_b >= n_early)
    def _():
        whole_sum()

    each(n_blk, back_from(True))
    inverse, coupling = invert(gram_ref[0 : 3 * k] * inv_count, k)
    inverse_ref[...] = inverse
    coupling_ref[...] = coupling
    each(n_grp // 2, lambda d: t_z(d).wait())
    image_ref[pl.ds(pl.multiple_of(core * half, 8), half)] = add_up(z_t, n_grp // 2)
    own_half = half_of(image_ref, core)
    back = remote(own_half, own_half, mate_send.at[1], mate_recv.at[1], mate, me_b)
    back.start()
    each(n_blk, back_from(False))
    each(n_blk, lambda d: chunk_back(d, me_b).wait_send())
    each(n_blk, lambda d: chunk_out(d)[1].wait_send())
    back.wait()


def first_kernel(mesh, items, tiles, cols, scales, x, p):
    n_grp, n_blk = mesh.shape["grp"], mesh.shape["blk"]
    side = 4
    k, here = x.shape
    rows_here, slots, width, _ = tiles.shape
    outer = rows_here * (slots // 8)
    vmem = pl.BlockSpec(memory_space=pltpu.VMEM)
    hbm = pl.BlockSpec(memory_space=pl.ANY)
    dma = pltpu.SemaphoreType.DMA
    across = pltpu.VMEM((2, outer, k, width), BF16)
    panel = pltpu.VMEM((rows_here, side, side, k, width), BF16)
    return pl.pallas_call(
        functools.partial(collect, n_grp, n_blk, side, 1.0 / items),
        out_shape=(
            jax.ShapeDtypeStruct((4 * k, 4 * k), F32),
            jax.ShapeDtypeStruct((k, 4 * k), F32),
            jax.ShapeDtypeStruct((3 * k, 4 * k), F32),
            jax.ShapeDtypeStruct((k, k), F32),
            jax.ShapeDtypeStruct((k, here), F32),
        ),
        in_specs=[hbm] * 5,
        out_specs=(vmem,) * 5,
        scratch_shapes=[
            pltpu.SMEM(cols.shape, jnp.int32),
            pltpu.SMEM(cols.shape, F32),
            pltpu.VMEM(x.shape, F32),
            pltpu.VMEM(x.shape, F32),
            pltpu.VMEM(tiles.shape, BF16),
            panel,
            panel,
            panel,
            pltpu.SMEM((2, *cols.shape), jnp.int32),
            across,
            across,
            across,
            across,
            across,
            across,
            pltpu.VMEM((4 * k, 4 * k), F32),
            pltpu.VMEM((n_blk, 8, 4 * k), F32),
            pltpu.VMEM((n_grp, 8, 4 * k), F32),
            pltpu.VMEM((k, 4 * k), F32),
            pltpu.VMEM((k // 2, 4 * k), F32),
            pltpu.VMEM((n_blk, k // 2, 4 * k), F32),
            pltpu.VMEM((n_grp // 2, k // 2, 4 * k), F32),
            dma((4 + rows_here,)),
            dma((2,)),
            dma((2,)),
            dma((2, side + 1, side)),
            dma((2, side + 1, side)),
            dma((2, side)),
            dma((2, side)),
            dma((2, side)),
            dma((2, side)),
            dma((2, side + 1, side)),
            dma((2, side + 1, side)),
            dma((6,)),
            dma((6,)),
            dma((n_blk,)),
            dma((n_blk,)),
            dma((n_grp,)),
            dma((n_grp,)),
            dma((n_blk,)),
            dma((n_blk,)),
            dma((2,)),
            dma((2,)),
            dma((n_blk,)),
            dma((n_blk,)),
            dma((n_grp // 2,)),
            dma((n_grp // 2,)),
        ],
        compiler_params=pltpu.CompilerParams(
            collective_id=0, has_side_effects=True, vmem_limit_bytes=56 * 2**20
        ),
        name="spread_and_mix",
    )(cols, scales, x, p, tiles)


def combine(
    inv_count,
    gram_ref,
    image_ref,
    inverse_ref,
    coupling_ref,
    s_ref,
    x_hbm,
    p_hbm,
    xn_ref,
    pn_ref,
    rows_ref,
    load_sem,
):
    k = s_ref.shape[0]
    n = 3 * k
    load = [
        pltpu.make_async_copy(x_hbm, rows_ref.at[0:k], load_sem.at[0]),
        pltpu.make_async_copy(p_hbm, rows_ref.at[2 * k : n], load_sem.at[1]),
    ]
    for copy in load:
        copy.start()
    rows_ref[k : 2 * k] = s_ref[...]
    gram = gram_ref[...] * inv_count
    on_t = (image_ref[...] * inv_count)[:, :n]
    basis = gram[:n, :n]
    raw = jnp.concatenate([basis[:, k : 2 * k], on_t.T, gram[n:, :n].T], axis=1)
    images = 0.5 * (raw + raw.T)

    operator = dot_nn(inverse_ref[:, :n], images)

    here = lax.broadcasted_iota(jnp.int32, (n, n), 0) == lax.broadcasted_iota(jnp.int32, (n, n), 1)
    shift = jnp.sum(jnp.where(here, operator, 0.0), keepdims=True) * (1.0 / n)
    centred = operator - jnp.where(here, jnp.broadcast_to(shift, (n, n)), 0.0)
    size = jnp.sum(centred * centred.T, keepdims=True)
    iterate = centred * jnp.broadcast_to(lax.rsqrt(size + 1e-6), (n, n))
    for _ in range(NS_STEPS - 1):
        iterate = 1.5 * iterate - 0.5 * dot_nn(iterate, dot_nn(iterate, iterate))
    first = iterate[:, :k]
    first = 1.5 * first - 0.5 * dot_nn(iterate, dot_nn(iterate, first))
    coefficients = 0.5 * (jnp.where(here[:, :k], 1.0, 0.0) + first)

    for copy in load:
        copy.wait()
    members = rows_ref[...]
    flat = coefficients.T
    gram_new = dot_nn(flat, dot_nn(basis, coefficients))
    both = jnp.concatenate([gram_new, flat], axis=1)
    lanes = both.shape[1]
    rows = [both[8 * q : 8 * q + 8] for q in range(k // 8)]
    sub = lax.broadcasted_iota(jnp.int32, (8, lanes), 0)
    scale = [None] * (k // 8)
    for start in range(0, k, PANEL):
        first = start // 8
        below = range(first, k // 8)
        panel = [{g: column(rows[g], start + c, lanes) for g in below} for c in range(PANEL)]
        for c in range(PANEL):
            q, r = (start + c) // 8, (start + c) % 8
            pivot = spread_row(panel[c][q], r)
            inv = 1.0 / pivot
            root = lax.rsqrt(pivot)
            scale[q] = root if r == 0 else jnp.where(sub == r, root, scale[q])
            here = {
                g: jnp.where(sub <= r, 0.0, panel[c][g]) if g == q else panel[c][g] for g in below
            }
            for later in range(c + 1, PANEL):
                factor = spread_row(panel[later][q], r) * inv
                panel[later] = {g: panel[later][g] - here[g] * factor for g in below}
            row = spread_row(rows[q], r) * inv
            for g in below:
                rows[g] = rows[g] - here[g] * row
    solved = jnp.concatenate([rows[g] * scale[g] for g in range(k // 8)], axis=0)[:, k:]

    on_residual = solved[:, k : 2 * k]
    back = dot_nt(on_residual, coupling_ref[...], HIGH)
    weights = jnp.concatenate(
        [solved, jnp.concatenate([-back, solved[:, k:]], axis=1)], axis=0
    )
    out = dot_nn(weights, members)
    xn_ref[...] = out[:k]
    pn_ref[...] = out[k:]


def second_kernel(items, gram, image, inverse, coupling, s, x, p):
    vmem = pl.BlockSpec(memory_space=pltpu.VMEM)
    hbm = pl.BlockSpec(memory_space=pl.ANY)
    return pl.pallas_call(
        functools.partial(combine, 1.0 / items),
        out_shape=(
            jax.ShapeDtypeStruct(x.shape, F32),
            jax.ShapeDtypeStruct(p.shape, F32),
        ),
        in_specs=[vmem] * 5 + [hbm] * 2,
        out_specs=(vmem, vmem),
        scratch_shapes=[
            pltpu.VMEM((3 * x.shape[0], x.shape[1]), F32),
            pltpu.SemaphoreType.DMA((2,)),
        ],
        compiler_params=pltpu.CompilerParams(vmem_limit_bytes=56 * 2**20),
        name="rayleigh_ritz",
    )(gram, image, inverse, coupling, s, x, p)


def solution(mesh):
    def per_device(tiles, cols, scales, x, p):
        items = x.shape[1] * mesh.shape["grp"] * mesh.shape["blk"]
        sums = first_kernel(mesh, items, tiles, cols, scales, x, p)
        return second_kernel(items, *sums, x, p)

    placed = (
        P(("grp", "blk"), None, None, None),
        P(("grp", "blk"), None),
        P(("grp", "blk"), None),
        P(None, ("grp", "blk")),
        P(None, ("grp", "blk")),
    )
    return jax.shard_map(
        per_device,
        mesh=mesh,
        in_specs=placed,
        out_specs=(P(None, ("grp", "blk")), P(None, ("grp", "blk"))),
        check_vma=False,
    )
```

```python
import functools

import jax
import jax.numpy as jnp
from jax import lax
from jax.experimental import pallas as pl
from jax.experimental.pallas import tpu as pltpu
from jax.sharding import PartitionSpec as P

NS_STEPS = 8
PANEL = 8
HIGH = lax.Precision.HIGHEST
F32 = jnp.float32
BF16 = jnp.bfloat16


def dot_nt(a, b, precision=None):
    return lax.dot_general(
        a, b, (((1,), (1,)), ((), ())), precision=precision, preferred_element_type=F32
    )


def dot_nn(a, b, precision=HIGH):
    return jnp.dot(a, b, precision=precision, preferred_element_type=F32)


def column(a, j, lanes):
    return jnp.broadcast_to(a[:, j : j + 1], (a.shape[0], lanes))


def spread_row(a, r):
    return jnp.broadcast_to(a[r : r + 1], a.shape)


def invert(gram, k):
    n, lanes = gram.shape[0], 128
    groups = n // PANEL
    sub = lax.broadcasted_iota(jnp.int32, (PANEL, lanes), 0)
    lane = lax.broadcasted_iota(jnp.int32, (PANEL, lanes), 1)
    left = [gram[PANEL * g : PANEL * g + PANEL] for g in range(groups)]
    right = [jnp.where(lane == sub + PANEL * g, 1.0, 0.0) for g in range(groups)]

    def turn(_, both):
        left, right = list(both[:groups]), list(both[groups:])
        panel = [[column(left[g], c, lanes) for g in range(groups)] for c in range(PANEL)]
        pivots = None
        for c in range(PANEL):
            inv = 1.0 / spread_row(panel[c][0], c)
            pivots = inv if c == 0 else jnp.where(sub == c, inv, pivots)
            here = [jnp.where(sub == c, 0.0, panel[c][0]), *panel[c][1:]]
            for later in range(c + 1, PANEL):
                factor = spread_row(panel[later][0], c) * inv
                panel[later] = [panel[later][g] - here[g] * factor for g in range(groups)]
            row_left = spread_row(left[0], c) * inv
            row_right = spread_row(right[0], c) * inv
            left = [left[g] - here[g] * row_left for g in range(groups)]
            right = [right[g] - here[g] * row_right for g in range(groups)]
        left[0], right[0] = left[0] * pivots, right[0] * pivots
        left = [pltpu.roll(a, lanes - PANEL, 1) for a in left]
        return (*left[1:], left[0], *right[1:], right[0])

    turns = k // PANEL
    both = lax.fori_loop(0, turns, turn, (*left, *right))
    coupling = jnp.concatenate(both[groups - turns : groups], axis=0)[:, :k]
    both = lax.fori_loop(turns, groups, turn, both)
    return jnp.concatenate(both[groups:], axis=0), coupling


def collect(
    n_grp,
    n_blk,
    side,
    inv_count,
    cols_hbm,
    scales_hbm,
    x_hbm,
    p_hbm,
    tiles_hbm,
    gram_ref,
    image_ref,
    inverse_ref,
    coupling_ref,
    s_ref,
    cols,
    scales,
    x_ref,
    p_ref,
    tiles,
    x_panel,
    p_panel,
    s_panel,
    wanted,
    x_out,
    x_in,
    p_out,
    p_in,
    s_out,
    s_in,
    partial,
    rs_buf,
    ar_buf,
    mine_t,
    mate_t,
    blk_t,
    z_t,
    load_sem,
    ask_send,
    ask_recv,
    x_send,
    x_recv,
    p_send,
    p_recv,
    p_send2,
    p_recv2,
    s_send,
    s_recv,
    z_send,
    z_recv,
    rs_send,
    rs_recv,
    ar_send,
    ar_recv,
    ag_send,
    ag_recv,
    mate_send,
    mate_recv,
    blk_send,
    blk_recv,
    zt_send,
    zt_recv,
):
    me_g = lax.axis_index("grp")
    me_b = lax.axis_index("blk")
    me_x, me_y = me_b // side, lax.rem(me_b, side)
    nxt = lax.rem(me_g + 1, n_grp)
    prv = lax.rem(me_g + n_grp - 1, n_grp)
    core = lax.rem(me_g, 2)
    mate = me_g + 1 - 2 * core
    rows_here, slots = cols.shape
    k = x_ref.shape[0]
    width = tiles.shape[2]
    cluster = n_blk * rows_here
    inner = 3 * slots // 4
    outer = slots // 8
    n_early = 3 * k // 8
    half = k // 2

    def load(src, dst, i):
        return pltpu.make_async_copy(src, dst, load_sem.at[i])

    load_x, load_p = load(x_hbm, x_ref, 0), load(p_hbm, p_ref, 1)
    load_small = [load(cols_hbm, cols, 2), load(scales_hbm, scales, 3)]
    load_tiles = [load(tiles_hbm.at[i], tiles.at[i], 4 + i) for i in range(rows_here)]
    load_x.start()
    barrier = pltpu.get_barrier_semaphore()

    def greet(grp, blk):
        pl.semaphore_signal(
            barrier, inc=1, device_id=(grp, blk), device_id_type=pl.DeviceIdType.MESH
        )

    def greet_blk(d, c):
        greet(me_g, lax.rem(me_b + d, n_blk))
        return c

    def greet_grp(d, c):
        greet(lax.rem(me_g + d, n_grp), me_b)
        return c

    lax.fori_loop(1, n_blk, greet_blk, 0)
    lax.fori_loop(1, n_grp, greet_grp, 0)
    for copy in [*load_small, load_p, *load_tiles]:
        copy.start()

    def block(ref, i):
        return ref[:, i * width : (i + 1) * width].astype(BF16)

    load_x.wait()
    for i in range(rows_here):
        x_panel[i, me_x, me_y] = block(x_ref, i)
    pl.semaphore_wait(barrier, n_blk - 1 + n_grp - 1)

    def remote(src, dst, send, recv, grp, blk):
        return pltpu.make_async_remote_copy(
            src_ref=src,
            dst_ref=dst,
            send_sem=send,
            recv_sem=recv,
            device_id=(grp, blk),
            device_id_type=pl.DeviceIdType.MESH,
        )

    ask = [
        remote(cols, wanted.at[0], ask_send.at[0], ask_recv.at[0], prv, me_b),
        remote(cols, wanted.at[1], ask_send.at[1], ask_recv.at[1], nxt, me_b),
    ]

    def each(count, act):
        def body(d, c):
            act(d)
            return c

        lax.fori_loop(1, count, body, 0)

    def along_x(d):
        return lax.rem(me_x + d, side) * side + me_y

    def along_y(d):
        return me_x * side + lax.rem(me_y + d, side)

    def p_first(d):
        a, b = p_panel.at[0, me_x, me_y], p_panel.at[1, me_x, me_y]
        return [
            remote(a, a, p_send.at[0, d], p_recv.at[0, d], me_g, along_x(d)),
            remote(b, b, p_send.at[1, d], p_recv.at[1, d], me_g, along_y(d)),
        ]

    def p_second(d):
        a, b = p_panel.at[0, :, me_y], p_panel.at[1, me_x]
        return [
            remote(a, a, p_send2.at[0, d], p_recv2.at[0, d], me_g, along_y(d)),
            remote(b, b, p_send2.at[1, d], p_recv2.at[1, d], me_g, along_x(d)),
        ]

    def near(buf, send, recv, d):
        a, b = buf.at[0, me_x, me_y], buf.at[1, me_x, me_y]
        return [
            remote(a, a, send.at[0, side, d], recv.at[0, side, d], me_g, along_x(d)),
            remote(b, b, send.at[1, side, d], recv.at[1, side, d], me_g, along_y(d)),
        ]

    def onward(buf, send, recv, e, d):
        from_x, from_y = lax.rem(me_x + side - e, side), lax.rem(me_y + side - e, side)
        a, b = buf.at[0, from_x, me_y], buf.at[1, me_x, from_y]
        return [
            remote(a, a, send.at[0, e, d], recv.at[0, e, d], me_g, along_y(d)),
            remote(b, b, send.at[1, e, d], recv.at[1, e, d], me_g, along_x(d)),
        ]

    def start(copies):
        for copy in copies:
            copy.start()

    def wait(copies):
        for copy in copies:
            copy.wait()

    def send_own(buf, send, recv):
        each(side, lambda d: start(near(buf, send, recv, d)))
        each(side, lambda d: start(onward(buf, send, recv, 0, d)))

    def send_own_row(buf, send, recv, i):
        each(side, lambda d: near(buf, send, recv, d)[i].start())
        each(side, lambda d: onward(buf, send, recv, 0, d)[i].start())

    def pass_on(buf, send, recv):
        def arrived(e):
            for copy in near(buf, send, recv, e):
                copy.wait_recv()
            each(side, lambda d: start(onward(buf, send, recv, e, d)))

        each(side, arrived)

    def all_in(buf, send, recv):
        def sent(d):
            for copy in near(buf, send, recv, d):
                copy.wait_send()
            wait(onward(buf, send, recv, 0, d))

        each(side, sent)
        each(side, lambda e: each(side, lambda d: wait(onward(buf, send, recv, e, d))))

    def crossed(buf):
        def get(c):
            c = lax.rem(c, cluster)
            at = c // rows_here
            return buf[lax.rem(c, rows_here), at // side, lax.rem(at, side)]

        return get

    away = 1 - core

    def exchange(out, into, at, side):
        return remote(
            out.at[side],
            into.at[side],
            z_send.at[at + side],
            z_recv.at[at + side],
            jnp.where(side == 0, nxt, prv),
            me_b,
        )

    def hand_over(get, out, into, at):
        copies = [exchange(out, into, at, side) for side in (away, 1 - away)]
        for side, copy in zip((away, 1 - away), copies):
            for i in range(rows_here):
                for j in range(outer):
                    slot = inner + side * outer + j
                    out[side, i * outer + j] = get(wanted[side, i, slot])
            copy.start()
        return copies

    def mix_inner(get):
        sums = []
        for i in range(rows_here):

            def body(j, acc, i=i):
                return acc + dot_nt(get(cols[i, j]), tiles[i, j]) * scales[i, j]

            sums.append(lax.fori_loop(0, inner, body, jnp.zeros((k, width), F32), unroll=24))
        return sums

    def mix_outer_row(total, into, i):
        for j in range(outer):
            a, b = inner + j, inner + outer + j
            total += dot_nt(into[0, i * outer + j], tiles[i, a]) * scales[i, a]
            total += dot_nt(into[1, i * outer + j], tiles[i, b]) * scales[i, b]
        return total

    def mix_outer(sums, into):
        return [mix_outer_row(sums[i], into, i) for i in range(rows_here)]

    send_own(x_panel, x_send, x_recv)
    wait(load_small)
    start(ask)
    load_p.wait()
    for i in range(rows_here):
        p_panel[i, me_x, me_y] = block(p_ref, i)
    pass_on(x_panel, x_send, x_recv)
    for d in range(1, side):
        for copy in p_first(d):
            copy.start()
    for copy in ask:
        copy.wait()
    all_in(x_panel, x_send, x_recv)
    x_across = hand_over(crossed(x_panel), x_out, x_in, 0)
    for d in range(1, side):
        for copy in p_first(d):
            copy.wait()
    for d in range(1, side):
        for copy in p_second(d):
            copy.start()
    for copy in load_tiles:
        copy.wait()
    sums = mix_inner(crossed(x_panel))
    for copy in x_across:
        copy.wait()
    for i in range(rows_here):
        total = mix_outer_row(sums[i], x_in, i)
        s_panel[i, me_x, me_y] = total.astype(BF16)
        send_own_row(s_panel, s_send, s_recv, i)
        s_ref[:, i * width : (i + 1) * width] = total

    basis = jnp.concatenate([x_ref[...], s_ref[...], p_ref[...]], axis=0)
    partial[0 : 3 * k, 0 : 3 * k] = dot_nt(basis, basis, HIGH)
    partial[0 : 3 * k, 3 * k :] = jnp.zeros((3 * k, k), F32)
    partial[3 * k :, 3 * k :] = jnp.zeros((k, k), F32)

    def chunk_out(d):
        to = lax.rem(me_b + d, n_blk)
        src = partial.at[pl.ds(pl.multiple_of(to * 8, 8), 8)]
        return to, remote(src, rs_buf.at[me_b], rs_send.at[d], rs_recv.at[d], me_g, to)

    def rs_start(d):
        to, copy = chunk_out(d)

        @pl.when(to < n_early)
        def _():
            copy.start()

    def rs_start_late(d):
        to, copy = chunk_out(d)

        @pl.when(to >= n_early)
        def _():
            copy.start()

    def add_up(buf, count):
        total = buf[0]
        for i in range(1, count):
            total += buf[i]
        return total

    def across(d):
        own = ar_buf.at[me_g]
        return remote(own, own, ar_send.at[d], ar_recv.at[d], lax.rem(me_g + d, n_grp), me_b)

    def cluster_sum():
        rs_buf[me_b] = partial[pl.ds(pl.multiple_of(me_b * 8, 8), 8)]
        each(n_blk, lambda d: chunk_out(d)[1].wait_recv())
        ar_buf[me_g] = add_up(rs_buf, n_blk)
        each(n_grp, lambda d: across(d).start())

    def rows_of(b):
        return gram_ref.at[pl.ds(pl.multiple_of(b * 8, 8), 8)]

    def chunk_back(d, who):
        return remote(
            rows_of(who), rows_of(who), ag_send.at[d], ag_recv.at[d], me_g, lax.rem(me_b + d, n_blk)
        )

    def whole_sum():
        each(n_grp, lambda d: across(d).wait())
        gram_ref[pl.ds(pl.multiple_of(me_b * 8, 8), 8)] = add_up(ar_buf, n_grp)
        each(n_blk, lambda d: chunk_back(d, me_b).start())

    each(n_blk, rs_start)

    for d in range(1, side):
        for copy in p_second(d):
            copy.wait()
    p_across = hand_over(crossed(p_panel), p_out, p_in, 2)
    pass_on(s_panel, s_send, s_recv)
    sums = mix_inner(crossed(p_panel))
    wait(p_across)
    u = jnp.concatenate(mix_outer(sums, p_in), axis=1)
    partial[3 * k :, 0 : 3 * k] = dot_nt(u, basis, HIGH)
    each(n_blk, rs_start_late)
    all_in(s_panel, s_send, s_recv)
    s_across = hand_over(crossed(s_panel), s_out, s_in, 4)

    @pl.when(me_b < n_early)
    def _():
        cluster_sum()

    sums = mix_inner(crossed(s_panel))
    wait(s_across)
    t = jnp.concatenate(mix_outer(sums, s_in), axis=1)
    mine_t[:, 0 : 3 * k] = dot_nt(t, basis, HIGH)
    mine_t[:, 3 * k :] = jnp.zeros((k, k), F32)

    def half_of(ref, c):
        return ref.at[pl.ds(pl.multiple_of(c * half, 8), half)]

    to_mate = remote(half_of(mine_t, 1 - core), mate_t, mate_send.at[0], mate_recv.at[0], mate, me_b)
    to_mate.start()

    @pl.when(me_b >= n_early)
    def _():
        cluster_sum()

    to_mate.wait()
    blk_t[me_b] = mine_t[pl.ds(pl.multiple_of(core * half, 8), half)] + mate_t[...]

    def t_blk(d):
        own = blk_t.at[me_b]
        return remote(own, own, blk_send.at[d], blk_recv.at[d], me_g, lax.rem(me_b + d, n_blk))

    each(n_blk, lambda d: t_blk(d).start())

    @pl.when(me_b < n_early)
    def _():
        whole_sum()

    def back_from(early):
        def arrived(d):
            source = lax.rem(me_b + n_blk - d, n_blk)

            @pl.when((source < n_early) if early else (source >= n_early))
            def _():
                chunk_back(d, source).wait_recv()

        return arrived

    each(n_blk, lambda d: t_blk(d).wait())
    z_t[me_g // 2] = add_up(blk_t, n_blk)

    def t_z(d):
        own = z_t.at[me_g // 2]
        return remote(own, own, zt_send.at[d], zt_recv.at[d], lax.rem(me_g + 2 * d, n_grp), me_b)

    each(n_grp // 2, lambda d: t_z(d).start())

    @pl.when(me_b >= n_early)
    def _():
        whole_sum()

    each(n_blk, back_from(True))
    inverse, coupling = invert(gram_ref[0 : 3 * k] * inv_count, k)
    inverse_ref[...] = inverse
    coupling_ref[...] = coupling
    each(n_grp // 2, lambda d: t_z(d).wait())
    image_ref[pl.ds(pl.multiple_of(core * half, 8), half)] = add_up(z_t, n_grp // 2)
    own_half = half_of(image_ref, core)
    back = remote(own_half, own_half, mate_send.at[1], mate_recv.at[1], mate, me_b)
    back.start()
    each(n_blk, back_from(False))
    each(n_blk, lambda d: chunk_back(d, me_b).wait_send())
    each(n_blk, lambda d: chunk_out(d)[1].wait_send())
    back.wait()


def first_kernel(mesh, items, tiles, cols, scales, x, p):
    n_grp, n_blk = mesh.shape["grp"], mesh.shape["blk"]
    side = 4
    k, here = x.shape
    rows_here, slots, width, _ = tiles.shape
    outer = rows_here * (slots // 8)
    vmem = pl.BlockSpec(memory_space=pltpu.VMEM)
    hbm = pl.BlockSpec(memory_space=pl.ANY)
    dma = pltpu.SemaphoreType.DMA
    across = pltpu.VMEM((2, outer, k, width), BF16)
    panel = pltpu.VMEM((rows_here, side, side, k, width), BF16)
    return pl.pallas_call(
        functools.partial(collect, n_grp, n_blk, side, 1.0 / items),
        out_shape=(
            jax.ShapeDtypeStruct((4 * k, 4 * k), F32),
            jax.ShapeDtypeStruct((k, 4 * k), F32),
            jax.ShapeDtypeStruct((3 * k, 4 * k), F32),
            jax.ShapeDtypeStruct((k, k), F32),
            jax.ShapeDtypeStruct((k, here), F32),
        ),
        in_specs=[hbm] * 5,
        out_specs=(vmem,) * 5,
        scratch_shapes=[
            pltpu.SMEM(cols.shape, jnp.int32),
            pltpu.SMEM(cols.shape, F32),
            pltpu.VMEM(x.shape, F32),
            pltpu.VMEM(x.shape, F32),
            pltpu.VMEM(tiles.shape, BF16),
            panel,
            panel,
            panel,
            pltpu.SMEM((2, *cols.shape), jnp.int32),
            across,
            across,
            across,
            across,
            across,
            across,
            pltpu.VMEM((4 * k, 4 * k), F32),
            pltpu.VMEM((n_blk, 8, 4 * k), F32),
            pltpu.VMEM((n_grp, 8, 4 * k), F32),
            pltpu.VMEM((k, 4 * k), F32),
            pltpu.VMEM((k // 2, 4 * k), F32),
            pltpu.VMEM((n_blk, k // 2, 4 * k), F32),
            pltpu.VMEM((n_grp // 2, k // 2, 4 * k), F32),
            dma((4 + rows_here,)),
            dma((2,)),
            dma((2,)),
            dma((2, side + 1, side)),
            dma((2, side + 1, side)),
            dma((2, side)),
            dma((2, side)),
            dma((2, side)),
            dma((2, side)),
            dma((2, side + 1, side)),
            dma((2, side + 1, side)),
            dma((6,)),
            dma((6,)),
            dma((n_blk,)),
            dma((n_blk,)),
            dma((n_grp,)),
            dma((n_grp,)),
            dma((n_blk,)),
            dma((n_blk,)),
            dma((2,)),
            dma((2,)),
            dma((n_blk,)),
            dma((n_blk,)),
            dma((n_grp // 2,)),
            dma((n_grp // 2,)),
        ],
        compiler_params=pltpu.CompilerParams(
            collective_id=0, has_side_effects=True, vmem_limit_bytes=56 * 2**20
        ),
        name="spread_and_mix",
    )(cols, scales, x, p, tiles)


def combine(
    inv_count,
    gram_ref,
    image_ref,
    inverse_ref,
    coupling_ref,
    s_ref,
    x_hbm,
    p_hbm,
    xn_ref,
    pn_ref,
    rows_ref,
    load_sem,
):
    k = s_ref.shape[0]
    n = 3 * k
    load = [
        pltpu.make_async_copy(x_hbm, rows_ref.at[0:k], load_sem.at[0]),
        pltpu.make_async_copy(p_hbm, rows_ref.at[2 * k : n], load_sem.at[1]),
    ]
    for copy in load:
        copy.start()
    rows_ref[k : 2 * k] = s_ref[...]
    gram = gram_ref[...] * inv_count
    on_t = (image_ref[...] * inv_count)[:, :n]
    basis = gram[:n, :n]
    raw = jnp.concatenate([basis[:, k : 2 * k], on_t.T, gram[n:, :n].T], axis=1)
    images = 0.5 * (raw + raw.T)

    operator = dot_nn(inverse_ref[:, :n], images)

    here = lax.broadcasted_iota(jnp.int32, (n, n), 0) == lax.broadcasted_iota(jnp.int32, (n, n), 1)
    shift = jnp.sum(jnp.where(here, operator, 0.0), keepdims=True) * (1.0 / n)
    centred = operator - jnp.where(here, jnp.broadcast_to(shift, (n, n)), 0.0)
    size = jnp.sum(centred * centred.T, keepdims=True)
    iterate = centred * jnp.broadcast_to(lax.rsqrt(size + 1e-6), (n, n))
    for _ in range(NS_STEPS - 1):
        iterate = 1.5 * iterate - 0.5 * dot_nn(iterate, dot_nn(iterate, iterate))
    first = iterate[:, :k]
    first = 1.5 * first - 0.5 * dot_nn(iterate, dot_nn(iterate, first))
    coefficients = 0.5 * (jnp.where(here[:, :k], 1.0, 0.0) + first)

    for copy in load:
        copy.wait()
    members = rows_ref[...]
    flat = coefficients.T
    gram_new = dot_nn(flat, dot_nn(basis, coefficients))
    both = jnp.concatenate([gram_new, flat], axis=1)
    lanes = both.shape[1]
    rows = [both[8 * q : 8 * q + 8] for q in range(k // 8)]
    sub = lax.broadcasted_iota(jnp.int32, (8, lanes), 0)
    scale = [None] * (k // 8)
    for start in range(0, k, PANEL):
        first = start // 8
        below = range(first, k // 8)
        panel = [{g: column(rows[g], start + c, lanes) for g in below} for c in range(PANEL)]
        for c in range(PANEL):
            q, r = (start + c) // 8, (start + c) % 8
            pivot = spread_row(panel[c][q], r)
            inv = 1.0 / pivot
            root = lax.rsqrt(pivot)
            scale[q] = root if r == 0 else jnp.where(sub == r, root, scale[q])
            here = {
                g: jnp.where(sub <= r, 0.0, panel[c][g]) if g == q else panel[c][g] for g in below
            }
            for later in range(c + 1, PANEL):
                factor = spread_row(panel[later][q], r) * inv
                panel[later] = {g: panel[later][g] - here[g] * factor for g in below}
            row = spread_row(rows[q], r) * inv
            for g in below:
                rows[g] = rows[g] - here[g] * row
    solved = jnp.concatenate([rows[g] * scale[g] for g in range(k // 8)], axis=0)[:, k:]

    on_residual = solved[:, k : 2 * k]
    back = dot_nt(on_residual, coupling_ref[...], HIGH)
    weights = jnp.concatenate(
        [solved, jnp.concatenate([-back, solved[:, k:]], axis=1)], axis=0
    )
    out = dot_nn(weights, members)
    xn_ref[...] = out[:k]
    pn_ref[...] = out[k:]


def second_kernel(items, gram, image, inverse, coupling, s, x, p):
    vmem = pl.BlockSpec(memory_space=pltpu.VMEM)
    hbm = pl.BlockSpec(memory_space=pl.ANY)
    return pl.pallas_call(
        functools.partial(combine, 1.0 / items),
        out_shape=(
            jax.ShapeDtypeStruct(x.shape, F32),
            jax.ShapeDtypeStruct(p.shape, F32),
        ),
        in_specs=[vmem] * 5 + [hbm] * 2,
        out_specs=(vmem, vmem),
        scratch_shapes=[
            pltpu.VMEM((3 * x.shape[0], x.shape[1]), F32),
            pltpu.SemaphoreType.DMA((2,)),
        ],
        compiler_params=pltpu.CompilerParams(vmem_limit_bytes=56 * 2**20),
        name="rayleigh_ritz",
    )(gram, image, inverse, coupling, s, x, p)


def solution(mesh):
    def per_device(tiles, cols, scales, x, p):
        items = x.shape[1] * mesh.shape["grp"] * mesh.shape["blk"]
        sums = first_kernel(mesh, items, tiles, cols, scales, x, p)
        return second_kernel(items, *sums, x, p)

    placed = (
        P(("grp", "blk"), None, None, None),
        P(("grp", "blk"), None),
        P(("grp", "blk"), None),
        P(None, ("grp", "blk")),
        P(None, ("grp", "blk")),
    )
    return jax.shard_map(
        per_device,
        mesh=mesh,
        in_specs=placed,
        out_specs=(P(None, ("grp", "blk")), P(None, ("grp", "blk"))),
        check_vma=False,
    )
```
